512 devices in a mesh: wide: 64 (over z_lo, x, y), narrow: 8 (over z_hi, core).
Axes of the slice: x: 4, y: 8, z: 8 (z_hi: 4, z_lo: 2; z = z_hi * 2 + z_lo), core: 2. Of those that a mesh axis runs over, the one named last changes fastest.
Arguments:
- users: bfloat16 [65536, 128], P('wide'), may hold values from -12 to 12
- items: bfloat16 [65536, 128], P(('wide', 'narrow')), may hold values from -12 to 12
- item_scale: bfloat16 [65536], P(('wide', 'narrow')), may hold values from 0.25 to 4
- user_mass: float32 [65536], P('wide'), may hold values from 0.5 to 2
- item_mass: float32 [65536], P(('wide', 'narrow')), may hold values from 0.5 to 2
Outputs:
- user_scale: float32 [65536], P('wide')
- item_scale_new: float32 [65536], P(('wide', 'narrow'))
The draws below stay inside these ranges and needn't reach their ends.
All inputs are finite; a program needn't handle non-finite values.
Results may differ from the reference program's by a relative error of at most 0.0003.
Values may be sent and summed in bfloat16 or wider, within the bound.
A program may use at most 64 MiB of HBM per device.

```python
import math
import jax
import jax.numpy as jnp
from jax import lax

D = 128
USERS = 65536
ITEMS = 65536


def topic_bank(key):
    return jnp.clip(jax.random.normal(key, (16, D), jnp.float32), -4.0, 4.0)


def topic_scales(key, rows):
    return jnp.exp(jax.random.uniform(key, (rows, 16), jnp.float32, math.log(0.15), math.log(1.5)))


def mixed_rows(bank, weights):
    total = jnp.zeros((weights.shape[0], D), jnp.float32)
    for topic in range(16):
        total = total + weights[:, topic:topic + 1] * bank[topic][None, :]
    return total


def draw_users(key, part):
    base = key
    key = jax.random.fold_in(key, 11)
    sign_key, scale_key, noise_key = jax.random.split(key, 3)
    bank = topic_bank(base)
    scales = topic_scales(scale_key, USERS)
    signs = jnp.clip(jax.random.normal(sign_key, (USERS, 16), jnp.float32), -4.0, 4.0)
    noise = jnp.clip(jax.random.normal(noise_key, (USERS, D), jnp.float32), -4.0, 4.0) * 1.6
    values = mixed_rows(bank, signs * scales) + noise
    return jnp.clip(values, -12.0, 12.0).astype(jnp.bfloat16)


def draw_items(key, part):
    base = key
    key = jax.random.fold_in(key, 23)
    sign_key, scale_key, noise_key = jax.random.split(key, 3)
    bank = topic_bank(base)
    scales = topic_scales(scale_key, ITEMS)
    signs = jnp.clip(jax.random.normal(sign_key, (ITEMS, 16), jnp.float32), -4.0, 4.0)
    noise = jnp.clip(jax.random.normal(noise_key, (ITEMS, D), jnp.float32), -4.0, 4.0) * 1.6
    values = mixed_rows(bank, signs * scales) + noise
    return jnp.clip(values, -12.0, 12.0).astype(jnp.bfloat16)


def steps_of(rng, shape, cuts, least, high):
    loudness = 1.0
    for position, parts in cuts:
        steps = jax.random.uniform(jax.random.fold_in(jax.random.fold_in(rng, 6), position), (parts,), jnp.float32, least / len(cuts), high / len(cuts))
        loudness = loudness * jnp.repeat(jnp.exp(steps), shape[position] // parts).reshape((-1,) + (1,) * (len(shape) - 1 - position))
    return loudness


def setup_inputs(seed: int = 0) -> dict:
    keys = jax.random.split(jax.random.key(seed), 6)
    return {
        "users": draw_users(jax.random.fold_in(keys[5], 71), 0),
        "items": draw_items(jax.random.fold_in(keys[5], 71), 0),
        "item_scale": jnp.clip(jnp.exp(math.log(4.0) - 2.7725887 * jax.random.uniform(keys[2], (ITEMS,), jnp.float32) ** steps_of(keys[2], (ITEMS,), ((0, 512),), -0.2, 0.2)), 0.25, 4.0).astype(jnp.bfloat16),
        "user_mass": jnp.clip(jnp.exp(math.log(2.0) - 1.3862944 * jax.random.uniform(keys[3], (USERS,), jnp.float32) ** steps_of(keys[3], (USERS,), ((0, 64),), -0.2, 0.2)), 0.5, 2.0),
        "item_mass": jnp.clip(jnp.exp(math.log(2.0) - 1.3862944 * jax.random.uniform(keys[4], (ITEMS,), jnp.float32) ** steps_of(keys[4], (ITEMS,), ((0, 512),), -0.2, 0.2)), 0.5, 2.0),
    }


def unit_rows(rows):
    values = rows.astype(jnp.float32)
    squares = lax.optimization_barrier(jnp.sum(values * values, axis=1, keepdims=True)) + 1e-06
    return (values * lax.rsqrt(squares)).astype(jnp.bfloat16)

def reference(users, items, item_scale, user_mass, item_mass):
    user_hat = unit_rows(users)
    item_hat = unit_rows(items)
    weights = item_scale.astype(jnp.float32)
    block = math.gcd(USERS, 1024)
    count = USERS // block

    def step(column_total, index):
        start = (index * block).astype(jnp.int32)
        rows = lax.dynamic_slice_in_dim(user_hat, start, block, 0)
        mass = lax.dynamic_slice_in_dim(user_mass, start, block, 0)
        scores = lax.dot_general(rows, item_hat, (((1,), (1,)), ((), ())), preferred_element_type=jnp.float32)
        kernel = jnp.exp(scores / 0.5)
        row_total = jnp.dot(kernel, weights, precision=lax.Precision.HIGHEST)
        scale = mass / (row_total / ITEMS)
        column_total = column_total + jnp.dot(scale, kernel, precision=lax.Precision.HIGHEST)
        return (column_total, scale)
    column_total, scales = lax.scan(step, jnp.zeros((ITEMS,), jnp.float32), jnp.arange(count, dtype=jnp.int32))
    user_scale = scales.reshape(USERS)
    item_scale_new = item_mass / (column_total / USERS)
    return (user_scale, item_scale_new)
```

```python
import functools
import math

import jax
import jax.numpy as jnp
from jax import lax
from jax.experimental import pallas as pl
from jax.experimental.pallas import tpu as pltpu
from jax.sharding import PartitionSpec as P

MESH = pl.DeviceIdType.MESH
F32 = jnp.float32
BF16 = jnp.bfloat16

NX, NY, NZ = 4, 8, 8
BLOCK = 128
HALF = 64
CHUNK = NX * BLOCK
USERS = 1024
TILE = 512
TILES = 2 * USERS // TILE
WIDTH = 128
SCALE = 2.0 * math.log2(math.e)


def unit_rows(values, axis):
    squares = jnp.sum(values * values, axis=axis, keepdims=True) + 1e-06
    return (values * lax.rsqrt(squares)).astype(BF16)


def body(
    item_count, user_count,
    users_ref, items_ref, weight_ref, user_mass_ref, item_mass_ref,
    user_scale_ref, item_scale_ref,
    rows, weights, bias, users, kernel, row_acc, row_parts, masses, user_rows, column_send,
    column_y, column_x,
    x_send, x_recv, y_send, y_recv, w_send, w_recv, u_send, u_recv, r_send, r_recv,
    cy_send, cy_recv, cx_send, cx_recv,
):
    wide = lax.axis_index("wide")
    narrow = lax.axis_index("narrow")
    z_lo, x, y = wide // (NX * NY), (wide // NY) % NX, wide % NY
    z_hi, core = narrow // 2, narrow % 2
    z = z_hi * 2 + z_lo
    line = z * 2 + core

    def plane(px, py):
        return (z_lo * (NX * NY) + px * NY + py, narrow)

    def column(pline):
        pz, pc = pline // 2, pline % 2
        return ((pz % 2) * (NX * NY) + x * NY + y, (pz // 2) * 2 + pc)

    def at_x(step):
        return plane((x + step) % NX, y)

    def at_y(step):
        return plane(x, (y + step) % NY)

    def at_line(step):
        return column((line + step) % (2 * NZ))

    barrier = pltpu.get_barrier_semaphore()

    def greet(partner):
        pl.semaphore_signal(barrier, inc=1, device_id=partner, device_id_type=MESH)

    def greet_x(step, carry):
        greet(at_x(step))
        return carry

    def greet_y(step, carry):
        greet(at_y(step))
        return carry

    def greet_line(step, carry):
        greet(at_line(step))
        return carry

    lax.fori_loop(1, NX, greet_x, 0)
    lax.fori_loop(1, NY, greet_y, 0)
    lax.fori_loop(1, 2 * NZ, greet_line, 0)

    hat = unit_rows(items_ref[...].astype(F32), 1)
    rows[y, 0, x] = hat[:HALF]
    rows[y, 1, x] = hat[HALF:]
    weights[y, x] = weight_ref[...].astype(F32)

    pl.semaphore_wait(barrier, NX - 1 + NY - 1 + 2 * NZ - 1)

    def remote(src, dst, send, recv, partner):
        return pltpu.make_async_remote_copy(
            src_ref=src, dst_ref=dst, send_sem=send, recv_sem=recv,
            device_id=partner, device_id_type=MESH,
        )

    def x_copies(step):
        source = (x - step) % NX
        out, back = [], []
        for half in (0, 1):
            out.append(remote(rows.at[y, half, x], rows.at[y, half, x],
                              x_send.at[step, half], x_recv.at[step, half], at_x(step)))
            back.append(remote(rows.at[y, half, source], rows.at[y, half, source],
                               x_send.at[step, half], x_recv.at[step, half], at_x(step)))
        out.append(remote(weights.at[y, x], weights.at[y, x],
                          x_send.at[step, 2], x_recv.at[step, 2], at_x(step)))
        back.append(remote(weights.at[y, source], weights.at[y, source],
                           x_send.at[step, 2], x_recv.at[step, 2], at_x(step)))
        return out, back

    for step in (1, 3, 2):
        for copy in x_copies(step)[0]:
            copy.start()

    ones = (lax.broadcasted_iota(jnp.int32, (WIDTH, TILE), 0) < 12).astype(F32).astype(BF16)
    for half in (0, 1):
        values = users_ref[half * TILE:(half + 1) * TILE, :].astype(F32).T
        users[z_lo * 2 + half, 0:WIDTH, :] = unit_rows(values, 0)
    for tile in range(TILES):
        users[tile, WIDTH:2 * WIDTH, :] = ones
    masses[z_lo] = user_mass_ref[...]

    z_up, z_down = at_line(2), at_line(2 * NZ - 2)

    def u_copies(block):
        out = []
        for half, partner in ((0, z_up), (1, z_down)):
            part = users.at[block * 2 + half, 0:WIDTH, :]
            out.append(remote(part, part, u_send.at[half], u_recv.at[half], partner))
        out.append(remote(masses.at[block], masses.at[block], u_send.at[2], u_recv.at[2], z_up))
        return out

    for copy in u_copies(z_lo):
        copy.start()

    for step in range(1, NX):
        for copy in x_copies(step)[1]:
            copy.wait_recv()

    def y_half(way, hop, source, half):
        part = rows.at[source, half]
        return remote(part, part, y_send.at[way, hop, half], y_recv.at[way, hop, half],
                      at_y(1 if way == 0 else NY - 1))

    def w_copy(source, step):
        part = weights.at[source]
        return remote(part, part, w_send.at[step], w_recv.at[step], at_y(step))

    for half in (0, 1):
        for way in (0, 1):
            y_half(way, 1, y, half).start()

    def send_weights(step, carry):
        w_copy(y, step).start()
        return carry

    lax.fori_loop(1, NY, send_weights, 0)

    row_acc[...] = jnp.zeros_like(row_acc)
    lane = lax.broadcasted_iota(jnp.int32, (BLOCK, BLOCK), 1)
    sub = lax.broadcasted_iota(jnp.int32, (8, BLOCK), 0)

    def make_bias(chunk):
        first = jnp.zeros((8, BLOCK), F32)
        second = jnp.zeros((8, BLOCK), F32)
        for block in range(NX):
            value = jnp.broadcast_to(0.5 * jnp.log(weights[chunk, block]), (8, BLOCK))
            high = value.astype(BF16).astype(F32)
            middle = (value - high).astype(BF16).astype(F32)
            low = value - high - middle
            first = jnp.where(sub == block, high, first)
            first = jnp.where(sub == block + 4, middle, first)
            second = jnp.where(sub == block, low, second)
        stacked = jnp.concatenate([first, second, jnp.zeros((BLOCK - 16, BLOCK), F32)], axis=0)
        turned = stacked.T
        for block in range(NX):
            own = jnp.where(lane % 4 == block, turned, 0.0).astype(BF16)
            bias[0, block] = own[:HALF]
            bias[1, block] = own[HALF:]

    def compute(chunk, first, last):
        def tile_step(tile, carry):
            left = jnp.concatenate(
                [rows[chunk].reshape(CHUNK, WIDTH), bias[...].reshape(CHUNK, WIDTH)], axis=1
            )
            scores = jnp.dot(left, users[tile], preferred_element_type=F32)
            values = jnp.exp2(scores * SCALE)
            kernel[chunk, tile] = values
            row_acc[tile] += jnp.sum(values.reshape(CHUNK // 8, 8, TILE), axis=0)
            return carry

        lax.fori_loop(first, last, tile_step, 0)

    make_bias(y)
    compute(y, z_lo * 2, z_lo * 2 + 2)
    for copy in u_copies(1 - z_lo):
        copy.wait_recv()
    compute(y, 2 - z_lo * 2, 4 - z_lo * 2)

    for hop in (1, 2, 3):
        behind, ahead = (y - hop) % NY, (y + hop) % NY
        for half in (0, 1):
            y_half(0, hop, behind, half).wait_recv()
            if hop < 3 or half == 0:
                y_half(0, hop + 1, behind, half).start()
            y_half(1, hop, ahead, half).wait_recv()
            if hop < 3 or half == 1:
                y_half(1, hop + 1, ahead, half).start()
        for source, step in ((behind, hop), (ahead, NY - hop)):
            w_copy(source, step).wait_recv()
            make_bias(source)
            compute(source, 0, TILES)
    far = (y + 4) % NY
    y_half(0, 4, far, 0).wait_recv()
    y_half(1, 4, far, 1).wait_recv()
    w_copy(far, 4).wait_recv()
    make_bias(far)
    compute(far, 0, TILES)

    for tile in range(TILES):
        total = jnp.sum(row_acc[tile], axis=0, keepdims=True)
        for part in range(TILE // 128):
            at = tile * (TILE // 128) + part
            row_parts[line, at:at + 1, :] = total[:, part * 128:(part + 1) * 128]

    def r_copy(source, step):
        part = row_parts.at[source]
        return remote(part, part, r_send.at[step], r_recv.at[step], at_line(step))

    def send_rows(step, carry):
        r_copy(line, step).start()
        return carry

    def wait_rows(step, carry):
        r_copy((line - step) % (2 * NZ), step).wait_recv()
        return carry

    lax.fori_loop(1, 2 * NZ, send_rows, 0)
    lax.fori_loop(1, 2 * NZ, wait_rows, 0)
    total = row_parts[0]
    for part in range(1, 2 * NZ):
        total = total + row_parts[part]
    scale = masses[...].reshape(16, 128) / (total / item_count)
    user_rows[...] = scale.reshape(2, 8, 128)
    user_scale_ref[...] = user_rows[z_lo]

    all_ones = jnp.ones((2 * WIDTH, WIDTH), BF16)
    diagonal = lax.broadcasted_iota(jnp.int32, (HALF, BLOCK), 0)
    across = lax.broadcasted_iota(jnp.int32, (HALF, BLOCK), 1)

    def cy_copy(source, target, step):
        return remote(column_send.at[target], column_y.at[source],
                      cy_send.at[step], cy_recv.at[step], at_y(step))

    def sum_columns(chunk):
        def block_step(block, carry):
            out = jnp.zeros((1, BLOCK), F32)
            for half in (0, 1):
                start = pl.multiple_of(half * (NX * HALF) + block * HALF, HALF)
                acc = jnp.zeros((HALF, 128), F32)
                for tile in range(TILES):
                    for part in range(TILE // 128):
                        at = tile * (TILE // 128) + part
                        scale_row = user_rows[at // 8, at % 8:at % 8 + 1, :]
                        piece = kernel[chunk, tile, pl.ds(start, HALF), part * 128:(part + 1) * 128]
                        acc = acc + piece * scale_row
                high = acc.astype(BF16)
                low = (acc - high.astype(F32)).astype(BF16)
                sums = jnp.dot(jnp.concatenate([high, low], axis=1), all_ones,
                               preferred_element_type=F32)
                kept = jnp.where(across == diagonal + half * HALF, sums, 0.0)
                out = out + jnp.sum(kept, axis=0, keepdims=True)
            column_send[chunk, block] = out
            return carry

        lax.fori_loop(0, NX, block_step, 0)

    def column_step(step, carry):
        target = (y + step) % NY
        sum_columns(target)

        @pl.when(step < NY)
        def _():
            cy_copy(y, target, step).start()

        return carry

    lax.fori_loop(1, NY + 1, column_step, 0)
    column_y[y] = column_send[y]

    def wait_y(step, carry):
        cy_copy((y - step) % NY, y, step).wait_recv()
        return carry

    lax.fori_loop(1, NY, wait_y, 0)
    total = column_y[0]
    for part in range(1, NY):
        total = total + column_y[part]
    column_x[NX] = total

    def cx_copy(source, target, step):
        return remote(column_x.at[NX, target], column_x.at[source, 0],
                      cx_send.at[step], cx_recv.at[step], at_x(step))

    for step in (1, 3, 2):
        cx_copy(x, (x + step) % NX, step).start()
    column_x[x, 0] = column_x[NX, x]
    for step in (1, 3, 2):
        cx_copy((x - step) % NX, x, step).wait_recv()
    total = column_x[0, 0]
    for part in range(1, NX):
        total = total + column_x[part, 0]
    item_scale_ref[...] = item_mass_ref[...] * weights[y, x] / (total / user_count)

    for step in range(1, NX):
        for copy in x_copies(step)[0]:
            copy.wait_send()
        cx_copy(x, (x + step) % NX, step).wait_send()
    for copy in u_copies(z_lo):
        copy.wait_send()
    for hop in (1, 2, 3, 4):
        behind, ahead = (y - hop + 1) % NY, (y + hop - 1) % NY
        for half in (0, 1):
            if hop < 4 or half == 0:
                y_half(0, hop, behind, half).wait_send()
            if hop < 4 or half == 1:
                y_half(1, hop, ahead, half).wait_send()

    def sent_y(step, carry):
        w_copy(y, step).wait_send()
        cy_copy(y, (y + step) % NY, step).wait_send()
        return carry

    def sent_rows(step, carry):
        r_copy(line, step).wait_send()
        return carry

    lax.fori_loop(1, NY, sent_y, 0)
    lax.fori_loop(1, 2 * NZ, sent_rows, 0)


def on_device(users, items, item_scale, user_mass, item_mass):
    user_count = users.shape[0] * lax.axis_size("wide")
    item_count = items.shape[0] * lax.axis_size("wide") * lax.axis_size("narrow")
    dma = pltpu.SemaphoreType.DMA
    vmem = pl.BlockSpec(memory_space=pltpu.VMEM)
    user_scale, item_scale_new = pl.pallas_call(
        functools.partial(body, item_count, user_count),
        out_shape=(
            jax.ShapeDtypeStruct((8, 128), F32),
            jax.ShapeDtypeStruct((1, 128), F32),
        ),
        in_specs=[vmem] * 5,
        out_specs=(vmem, vmem),
        scratch_shapes=[
            pltpu.VMEM((NY, 2, NX, HALF, WIDTH), BF16),
            pltpu.VMEM((NY, NX, 1, BLOCK), F32),
            pltpu.VMEM((2, NX, HALF, BLOCK), BF16),
            pltpu.VMEM((TILES, 2 * WIDTH, TILE), BF16),
            pltpu.VMEM((NY, TILES, CHUNK, TILE), F32),
            pltpu.VMEM((TILES, 8, TILE), F32),
            pltpu.VMEM((2 * NZ, 16, 128), F32),
            pltpu.VMEM((2, 8, 128), F32),
            pltpu.VMEM((2, 8, 128), F32),
            pltpu.VMEM((NY, NX, 1, BLOCK), F32),
            pltpu.VMEM((NY, NX, 1, BLOCK), F32),
            pltpu.VMEM((NX + 1, NX, 1, BLOCK), F32),
            dma((NX, 3)), dma((NX, 3)),
            dma((2, 5, 2)), dma((2, 5, 2)),
            dma((NY,)), dma((NY,)),
            dma((3,)), dma((3,)),
            dma((2 * NZ,)), dma((2 * NZ,)),
            dma((NY,)), dma((NY,)),
            dma((NX,)), dma((NX,)),
        ],
        compiler_params=pltpu.CompilerParams(
            collective_id=0, has_side_effects=True, vmem_limit_bytes=56 * 1024 * 1024
        ),
        cost_estimate=pl.CostEstimate(
            flops=2 * 4096 * 2048 * 256, bytes_accessed=1 << 20, transcendentals=4096 * 2048
        ),
        name="scaling",
    )(
        users,
        items,
        item_scale.reshape(1, 128),
        user_mass.reshape(8, 128),
        item_mass.reshape(1, 128),
    )
    return user_scale.reshape(1024), item_scale_new.reshape(128)


def solution(mesh):
    in_specs = (
        P("wide", None),
        P(("wide", "narrow"), None),
        P(("wide", "narrow")),
        P("wide"),
        P(("wide", "narrow")),
    )
    out_specs = (P("wide"), P(("wide", "narrow")))
    return jax.shard_map(
        on_device, mesh=mesh, in_specs=in_specs, out_specs=out_specs, check_vma=False
    )
```

```python
import functools
import math

import jax
import jax.numpy as jnp
from jax import lax
from jax.experimental import pallas as pl
from jax.experimental.pallas import tpu as pltpu
from jax.sharding import PartitionSpec as P

MESH = pl.DeviceIdType.MESH
F32 = jnp.float32
BF16 = jnp.bfloat16

NX, NY, NZ = 4, 8, 8
LINE = 2 * NZ
BLOCK = 128
HALF = 64
USERS = 1024
TILE = 512
TILES = 2 * USERS // TILE
PARTS = TILE // 128
WIDTH = 128
SCALE = 2.0 * math.log2(math.e)


def unit_rows(values, axis):
    squares = jnp.sum(values * values, axis=axis, keepdims=True) + 1e-06
    return (values * lax.rsqrt(squares)).astype(BF16)


def three_pieces(weight):
    value = 0.5 * jnp.log(weight)
    high = value.astype(BF16).astype(F32)
    middle = (value - high).astype(BF16).astype(F32)
    return high, middle, value - high - middle


def body(
    item_count,
    users_hbm, items_hbm, weight_hbm, mass_hbm,
    row_total_ref, column_total_ref,
    users_in, items_in, weight_in, rows, turned, users, kernel, row_acc, row_parts, masses,
    user_rows, column_send, column_y, column_x, column_half,
    in_sem, x_send, x_recv, y_send, y_recv, u_send, u_recv, r_send, r_recv,
    cy_send, cy_recv, cx_send, cx_recv,
):
    wide = lax.axis_index("wide")
    narrow = lax.axis_index("narrow")
    y = wide & (NY - 1)
    x = (wide >> 3) & (NX - 1)
    z_lo = wide >> 5
    line = ((narrow >> 1) << 2) | (z_lo << 1) | (narrow & 1)
    wide_no_y = wide - y
    wide_no_x = wide - (x << 3)
    wide_no_z = wide & (NX * NY - 1)

    def at_x(step):
        return (wide_no_x + (((x + step) & (NX - 1)) << 3), narrow)

    def at_y(step):
        return (wide_no_y + ((y + step) & (NY - 1)), narrow)

    def at_line(step):
        other = (line + step) & (LINE - 1)
        return (wide_no_z + (((other >> 1) & 1) << 5), ((other >> 2) << 1) | (other & 1))

    barrier = pltpu.get_barrier_semaphore()

    def greet(partner):
        pl.semaphore_signal(barrier, inc=1, device_id=partner, device_id_type=MESH)

    def greet_line(step, carry):
        greet(at_line(step))
        return carry

    for step in (1, 3, 2):
        greet(at_x(step))
    for step in (1, 7, 2, 6, 3, 5, 4):
        greet(at_y(step))
    lax.fori_loop(1, LINE, greet_line, 0)

    get_items = pltpu.make_async_copy(items_hbm, items_in, in_sem.at[0])
    get_weight = pltpu.make_async_copy(weight_hbm, weight_in, in_sem.at[1])
    get_users = pltpu.make_async_copy(users_hbm, users_in, in_sem.at[2])
    get_mass = pltpu.make_async_copy(mass_hbm, masses.at[z_lo], in_sem.at[3])
    get_items.start()
    get_weight.start()
    get_users.start()
    get_mass.start()

    get_items.wait()
    get_weight.wait()
    rows[0, x, 0:BLOCK, :] = unit_rows(items_in[...].astype(F32), 1)
    rows[0, x, BLOCK:BLOCK + 16, :] = jnp.broadcast_to(
        weight_in[...].astype(F32), (16, BLOCK)
    ).astype(BF16)

    pl.semaphore_wait(barrier, NX - 1 + NY - 1 + LINE - 1)

    def remote(src, dst, send, recv, partner):
        return pltpu.make_async_remote_copy(
            src_ref=src, dst_ref=dst, send_sem=send, recv_sem=recv,
            device_id=partner, device_id_type=MESH,
        )

    def settle(part, sem):
        pltpu.make_async_copy(part, part, sem).wait()

    for step in (1, 3, 2):
        remote(rows.at[0, x], rows.at[0, x], x_send.at[0], x_recv.at[0], at_x(step)).start()

    up, down = at_line(2), at_line(LINE - 2)
    get_users.wait()
    get_mass.wait()
    for half, partner in ((0, up), (1, down)):
        values = users_in[half * TILE:(half + 1) * TILE, :].astype(F32).T
        tile = z_lo * 2 + half
        users[tile, 0:WIDTH, :] = unit_rows(values, 0)
        part = users.at[tile, 0:WIDTH, :]
        remote(part, part, u_send.at[half], u_recv.at[half], partner).start()
    remote(masses.at[z_lo], masses.at[z_lo], u_send.at[2], u_recv.at[2], up).start()

    settle(rows.at[0, 0:3], x_recv.at[0])

    def slot_of(way, hop):
        return 7 if hop == 4 else max(2 * hop - 1 + way, 0) if hop else 0

    def y_copy(way, hop, half):
        pair = slice(2 * half, 2 * half + 2)
        return remote(
            rows.at[slot_of(way, hop - 1), pair], rows.at[slot_of(way, hop), pair],
            y_send.at[0], y_recv.at[way, hop, half], at_y(NY - 1 if way else 1),
        )

    for half in (0, 1):
        for way in (0, 1):
            y_copy(way, 1, half).start()

    ones = jnp.ones((WIDTH, TILE), BF16)
    for tile in range(TILES):
        users[tile, WIDTH:2 * WIDTH, :] = ones
    row_acc[...] = jnp.zeros_like(row_acc)

    sub = lax.broadcasted_iota(jnp.int32, (8, BLOCK), 0)

    def turn(slot):
        value = jnp.ones((8, BLOCK), F32)
        for block in range(NX):
            weight = rows[slot, block, BLOCK:BLOCK + 16, :].astype(F32)[0:8]
            value = jnp.where((sub & 3) == block, weight, value)
        high, middle, low = three_pieces(value)
        first = jnp.where(sub < 4, high, middle)
        second = jnp.where(sub < 4, low, 0.0)
        stacked = jnp.concatenate([first, second, jnp.zeros((BLOCK - 16, BLOCK), F32)], axis=0)
        turned[slot] = stacked.T.astype(BF16)

    lane = lax.broadcasted_iota(jnp.int32, (1, BLOCK), 1)

    def before(hop):
        if hop == 0:
            turn(0)
            return
        for half in (0, 1):
            for way in (0, 1):
                if hop < 4 or half == way:
                    y_copy(way, hop, half).wait_recv()
                if hop < 3 or (hop == 3 and half == way):
                    y_copy(way, hop + 1, half).start()
        for slot in sorted({slot_of(0, hop), slot_of(1, hop)}):
            turn(slot)

    def compute_step(at, carry):
        slot, later = at >> 1, at & 1
        for known, hop in ((0, 0), (2, 1), (6, 2), (10, 3), (14, 4)):
            @pl.when(at == known)
            def _():
                before(hop)

        @pl.when(at == 1)
        def _():
            for half in (0, 1):
                settle(users.at[half, 0:WIDTH, :], u_recv.at[half])
            settle(masses.at[0], u_recv.at[2])

        block_of_users = (z_lo + later) & 1
        accs = [jnp.zeros((8, TILE), F32) for _ in range(2)]
        bias = turned[slot]
        for block in range(NX):
            kept = ((lane & 3) == block).astype(F32).astype(BF16)
            left = jnp.concatenate([rows[slot, block, 0:BLOCK, :], bias * kept], axis=1)
            for part in range(2):
                tile = block_of_users * 2 + part
                scores = jnp.dot(left, users[tile], preferred_element_type=F32)
                values = jnp.exp2((scores * SCALE).astype(BF16))
                kernel[slot, tile, block * BLOCK:(block + 1) * BLOCK] = values
                accs[part] += jnp.sum(values.astype(F32).reshape(BLOCK // 8, 8, TILE), axis=0)
        for part in range(2):
            row_acc[block_of_users * 2 + part] += accs[part]
        return carry

    lax.fori_loop(0, 16, compute_step, 0)

    for tile in range(TILES):
        total = jnp.sum(row_acc[tile], axis=0, keepdims=True)
        for part in range(PARTS):
            at = tile * PARTS + part
            row_parts[line, at:at + 1, :] = total[:, part * 128:(part + 1) * 128]

    def send_rows(step, carry):
        remote(row_parts.at[line], row_parts.at[line], r_send.at[0], r_recv.at[0],
               at_line(step)).start()
        return carry

    lax.fori_loop(1, LINE, send_rows, 0)
    settle(row_parts.at[0:LINE - 1], r_recv.at[0])
    total = row_parts[0]
    for part in range(1, LINE):
        total = total + row_parts[part]
    scale = masses[...].reshape(16, 128) / (total / item_count)
    for at in range(TILES * PARTS):
        user_rows[at] = jnp.broadcast_to(scale[at:at + 1, :], (8, 128))
    column_half[...] = total.reshape(2, 8, 128)
    row_total_ref[...] = column_half[z_lo]

    def sum_columns(slot):
        for block in range(NX):
            pieces = []
            for half in (0, 1):
                acc = jnp.zeros((HALF // 8, 8, 128), F32)
                for tile in range(TILES):
                    for part in range(PARTS):
                        piece = kernel[slot, tile,
                                       block * BLOCK + half * HALF:block * BLOCK + (half + 1) * HALF,
                                       part * 128:(part + 1) * 128]
                        piece = piece.astype(F32).reshape(HALF // 8, 8, 128)
                        acc = acc + piece * user_rows[tile * PARTS + part]
                pieces.append(acc.reshape(HALF, 128))
            flat = jnp.concatenate(pieces, axis=0).T
            column_send[slot, block] = jnp.sum(flat, axis=0, keepdims=True)

    def column_step(step, carry):
        slot = step & (NY - 1)
        sum_columns(slot)
        hop = (step + 1) >> 1
        ahead = jnp.where((step & 1) == 0, hop, NY - hop)

        @pl.when(step < NY)
        def _():
            remote(column_send.at[slot], column_y.at[slot], cy_send.at[0], cy_recv.at[0],
                   at_y(ahead)).start()

        return carry

    lax.fori_loop(1, NY + 1, column_step, 0)
    column_y[0] = column_send[0]
    settle(column_y.at[1:NY], cy_recv.at[0])
    total = column_y[0]
    for part in range(1, NY):
        total = total + column_y[part]
    column_x[NX] = total

    for step in (1, 3, 2):
        remote(column_x.at[NX, (x + step) & (NX - 1)], column_x.at[step, 0],
               cx_send.at[0], cx_recv.at[0], at_x(step)).start()
    column_x[0, 0] = column_x[NX, x]
    settle(column_x.at[1:NX, 0], cx_recv.at[0])
    total = column_x[0, 0]
    for part in range(1, NX):
        total = total + column_x[part, 0]
    weight = weight_in[...].astype(F32)
    column_total_ref[...] = total / weight

    settle(rows.at[0, 0:3], x_send.at[0])
    settle(rows.at[0:7], y_send.at[0])
    for half in (0, 1):
        settle(users.at[half, 0:WIDTH, :], u_send.at[half])
    settle(masses.at[0], u_send.at[2])
    settle(row_parts.at[0:LINE - 1], r_send.at[0])
    settle(column_y.at[1:NY], cy_send.at[0])
    settle(column_x.at[1:NX, 0], cx_send.at[0])


def on_device(users, items, item_scale, user_mass, item_mass):
    user_count = users.shape[0] * lax.axis_size("wide")
    item_count = items.shape[0] * lax.axis_size("wide") * lax.axis_size("narrow")
    dma = pltpu.SemaphoreType.DMA
    vmem = pl.BlockSpec(memory_space=pltpu.VMEM)
    row_total, column_total = pl.pallas_call(
        functools.partial(body, item_count),
        out_shape=(
            jax.ShapeDtypeStruct((8, 128), F32),
            jax.ShapeDtypeStruct((1, 128), F32),
        ),
        in_specs=[pl.BlockSpec(memory_space=pl.ANY)] * 4,
        out_specs=(vmem, vmem),
        scratch_shapes=[
            pltpu.VMEM((USERS, WIDTH), BF16),
            pltpu.VMEM((BLOCK, WIDTH), BF16),
            pltpu.VMEM((1, BLOCK), BF16),
            pltpu.VMEM((NY, NX, BLOCK + 16, WIDTH), BF16),
            pltpu.VMEM((NY, BLOCK, BLOCK), BF16),
            pltpu.VMEM((TILES, 2 * WIDTH, TILE), BF16),
            pltpu.VMEM((NY, TILES, NX * BLOCK, TILE), BF16),
            pltpu.VMEM((TILES, 8, TILE), F32),
            pltpu.VMEM((LINE, 16, 128), F32),
            pltpu.VMEM((2, 8, 128), F32),
            pltpu.VMEM((TILES * PARTS, 8, 128), F32),
            pltpu.VMEM((NY, NX, 1, BLOCK), F32),
            pltpu.VMEM((NY, NX, 1, BLOCK), F32),
            pltpu.VMEM((NX + 1, NX, 1, BLOCK), F32),
            pltpu.VMEM((2, 8, 128), F32),
            dma((4,)),
            dma((1,)), dma((1,)),
            dma((1,)), dma((2, 5, 2)),
            dma((3,)), dma((3,)),
            dma((1,)), dma((1,)),
            dma((1,)), dma((1,)),
            dma((1,)), dma((1,)),
        ],
        compiler_params=pltpu.CompilerParams(
            collective_id=0, has_side_effects=True, vmem_limit_bytes=56 * 1024 * 1024
        ),
        cost_estimate=pl.CostEstimate(
            flops=2 * 4096 * 2048 * 256, bytes_accessed=1 << 20, transcendentals=4096 * 2048
        ),
        name="scaling",
    )(users, items, item_scale.reshape(1, 128), user_mass.reshape(8, 128))
    user_scale = user_mass / (row_total.reshape(1024) / item_count)
    item_scale_new = item_mass / (column_total.reshape(128) / user_count)
    return user_scale, item_scale_new


def solution(mesh):
    in_specs = (
        P("wide", None),
        P(("wide", "narrow"), None),
        P(("wide", "narrow")),
        P("wide"),
        P(("wide", "narrow")),
    )
    out_specs = (P("wide"), P(("wide", "narrow")))
    return jax.shard_map(
        on_device, mesh=mesh, in_specs=in_specs, out_specs=out_specs, check_vma=False
    )
```

```python
import functools
import math

import jax
import jax.numpy as jnp
from jax import lax
from jax.experimental import pallas as pl
from jax.experimental.pallas import tpu as pltpu
from jax.sharding import PartitionSpec as P

MESH = pl.DeviceIdType.MESH
F32 = jnp.float32
BF16 = jnp.bfloat16

NX, NY, NZ = 4, 8, 8
LINE = 2 * NZ
BLOCK = 128
USERS = 1024
TILE = 512
TILES = 2 * USERS // TILE
PARTS = TILE // 128
WIDTH = 128
SCALE = 2.0 * math.log2(math.e)


def unit_rows(values, axis):
    squares = jnp.sum(values * values, axis=axis, keepdims=True) + 1e-06
    return (values * lax.rsqrt(squares)).astype(BF16)


def two_pieces(value):
    high = value.astype(BF16)
    return high, (value - high.astype(F32)).astype(BF16)


def body(
    item_count,
    users_hbm, items_hbm, weight_hbm, mass_hbm,
    row_total_ref, column_total_ref,
    users_in, items_in, weight_in, rows, hats, users, kernel, row_acc, row_parts, masses,
    user_rows, column_send, column_y, column_x, column_half,
    in_sem, x_send, x_recv, y_send, y_recv, u_send, u_recv, r_send, r_recv,
    cy_send, cy_recv, cx_send, cx_recv,
):
    wide = lax.axis_index("wide")
    narrow = lax.axis_index("narrow")
    y = wide & (NY - 1)
    x = (wide >> 3) & (NX - 1)
    z_lo = wide >> 5
    line = ((narrow >> 1) << 2) | (z_lo << 1) | (narrow & 1)
    wide_no_y = wide - y
    wide_no_x = wide - (x << 3)
    wide_no_z = wide & (NX * NY - 1)

    def at_x(step):
        return (wide_no_x + (((x + step) & (NX - 1)) << 3), narrow)

    def at_y(step):
        return (wide_no_y + ((y + step) & (NY - 1)), narrow)

    def at_line(step):
        other = (line + step) & (LINE - 1)
        return (wide_no_z + (((other >> 1) & 1) << 5), ((other >> 2) << 1) | (other & 1))

    barrier = pltpu.get_barrier_semaphore()

    def greet(partner):
        pl.semaphore_signal(barrier, inc=1, device_id=partner, device_id_type=MESH)

    def greet_line(step, carry):
        greet(at_line(step))
        return carry

    for step in (1, 3, 2):
        greet(at_x(step))
    for step in (1, 7, 2, 6, 3, 5, 4):
        greet(at_y(step))
    lax.fori_loop(1, LINE, greet_line, 0)

    get_items = pltpu.make_async_copy(items_hbm, items_in, in_sem.at[0])
    get_weight = pltpu.make_async_copy(weight_hbm, weight_in, in_sem.at[1])
    get_users = pltpu.make_async_copy(users_hbm, users_in, in_sem.at[2])
    get_mass = pltpu.make_async_copy(mass_hbm, masses.at[z_lo], in_sem.at[3])
    get_items.start()
    get_weight.start()
    get_users.start()
    get_mass.start()

    get_items.wait()
    get_weight.wait()
    rows[0, x, 0:BLOCK, :] = unit_rows(items_in[...].astype(F32), 1)
    rows[0, x, BLOCK:BLOCK + 16, :] = jnp.broadcast_to(
        weight_in[...].astype(F32), (16, BLOCK)
    ).astype(BF16)

    pl.semaphore_wait(barrier, NX - 1 + NY - 1 + LINE - 1)

    def remote(src, dst, send, recv, partner):
        return pltpu.make_async_remote_copy(
            src_ref=src, dst_ref=dst, send_sem=send, recv_sem=recv,
            device_id=partner, device_id_type=MESH,
        )

    def settle(part, sem):
        pltpu.make_async_copy(part, part, sem).wait()

    for step in (1, 3, 2):
        remote(rows.at[0, x], rows.at[0, x], x_send.at[0], x_recv.at[0], at_x(step)).start()

    up, down = at_line(2), at_line(LINE - 2)
    get_users.wait()
    get_mass.wait()
    for half, partner in ((0, up), (1, down)):
        values = users_in[half * TILE:(half + 1) * TILE, :].astype(F32).T
        hats[z_lo * 2 + half] = unit_rows(values, 0)
        part = hats.at[z_lo * 2 + half]
        remote(part, part, u_send.at[half], u_recv.at[half], partner).start()
    remote(masses.at[z_lo], masses.at[z_lo], u_send.at[2], u_recv.at[2], up).start()

    settle(rows.at[0, 0:3], x_recv.at[0])

    def slot_of(way, hop):
        return 7 if hop == 4 else max(2 * hop - 1 + way, 0) if hop else 0

    def y_copy(way, hop, half):
        pair = slice(2 * half, 2 * half + 2)
        return remote(
            rows.at[slot_of(way, hop - 1), pair], rows.at[slot_of(way, hop), pair],
            y_send.at[0], y_recv.at[way, hop, half], at_y(NY - 1 if way else 1),
        )

    for half in (0, 1):
        for way in (0, 1):
            y_copy(way, 1, half).start()

    row_acc[...] = jnp.zeros_like(row_acc)

    def scale_users(block):
        for half in (0, 1):
            high, low = two_pieces(hats[block * 2 + half].astype(F32) * SCALE)
            users[block * 2 + half, 0:WIDTH, :] = high
            users[block * 2 + half, WIDTH:2 * WIDTH, :] = low

    scale_users(z_lo)

    def before(hop):
        for half in (0, 1):
            for way in (0, 1):
                if hop < 4 or half == way:
                    y_copy(way, hop, half).wait_recv()
                if hop < 3 or (hop == 3 and half == way):
                    y_copy(way, hop + 1, half).start()

    def compute_step(at, carry):
        slot, later = at >> 1, at & 1
        for known, hop in ((2, 1), (6, 2), (10, 3), (14, 4)):
            @pl.when(at == known)
            def _():
                before(hop)

        @pl.when(at == 1)
        def _():
            for half in (0, 1):
                settle(hats.at[half], u_recv.at[half])
            settle(masses.at[0], u_recv.at[2])
            scale_users(1 - z_lo)

        block_of_users = (z_lo + later) & 1
        accs = [jnp.zeros((16, TILE), F32) for _ in range(2)]
        for pair in range(NX // 2):
            both = (2 * pair, 2 * pair + 1)
            hat = jnp.concatenate([rows[slot, block, 0:BLOCK, :] for block in both], axis=0)
            left = jnp.concatenate([hat, hat], axis=1)
            weight = jnp.concatenate(
                [rows[slot, block, BLOCK:BLOCK + 16, :] for block in both], axis=1
            )
            for part in range(2):
                tile = block_of_users * 2 + part
                scores = jnp.dot(left, users[tile], preferred_element_type=F32)
                values = jnp.exp2(scores.astype(BF16))
                kernel[slot, tile, pair * 2 * BLOCK:(pair + 1) * 2 * BLOCK] = values
                accs[part] += jnp.dot(weight, values, preferred_element_type=F32)
        for part in range(2):
            row_acc[block_of_users * 2 + part] += accs[part][0:8]
        return carry

    lax.fori_loop(0, 16, compute_step, 0)

    for tile in range(TILES):
        total = row_acc[tile][0:1, :]
        for part in range(PARTS):
            at = tile * PARTS + part
            row_parts[line, at:at + 1, :] = total[:, part * 128:(part + 1) * 128]

    def send_rows(step, carry):
        remote(row_parts.at[line], row_parts.at[line], r_send.at[0], r_recv.at[0],
               at_line(step)).start()
        return carry

    lax.fori_loop(1, LINE, send_rows, 0)
    settle(row_parts.at[0:LINE - 1], r_recv.at[0])
    total = row_parts[0]
    for part in range(1, LINE):
        total = total + row_parts[part]
    scale = masses[...].reshape(16, 128) / (total / item_count)
    sub = lax.broadcasted_iota(jnp.int32, (16, 128), 0)
    high, low = two_pieces(scale)
    high, low = high.astype(F32), low.astype(F32)
    for at in range(TILES * PARTS):
        first = jnp.broadcast_to(high[at:at + 1, :], (16, 128))
        second = jnp.broadcast_to(low[at:at + 1, :], (16, 128))
        pieces = jnp.where(sub == 0, first, jnp.where(sub == 1, second, 0.0)).astype(BF16)
        user_rows[:, at * 128:(at + 1) * 128] = pieces
    column_half[...] = total.reshape(2, 8, 128)
    row_total_ref[...] = column_half[z_lo]

    def sum_columns(slot):
        sums = jnp.zeros((16, NX * BLOCK), F32)
        for tile in range(TILES):
            sums += lax.dot_general(
                user_rows[:, tile * TILE:(tile + 1) * TILE], kernel[slot, tile],
                (((1,), (1,)), ((), ())), preferred_element_type=F32,
            )
        flat = sums[0:1, :] + sums[1:2, :]
        for block in range(NX):
            column_send[slot, block] = flat[:, block * BLOCK:(block + 1) * BLOCK]

    def column_step(step, carry):
        slot = step & (NY - 1)
        sum_columns(slot)
        hop = (step + 1) >> 1
        ahead = jnp.where((step & 1) == 0, hop, NY - hop)

        @pl.when(step < NY)
        def _():
            remote(column_send.at[slot], column_y.at[slot], cy_send.at[0], cy_recv.at[0],
                   at_y(ahead)).start()

        return carry

    lax.fori_loop(1, NY + 1, column_step, 0)
    column_y[0] = column_send[0]
    settle(column_y.at[1:NY], cy_recv.at[0])
    total = column_y[0]
    for part in range(1, NY):
        total = total + column_y[part]
    column_x[NX] = total

    for step in (1, 3, 2):
        remote(column_x.at[NX, (x + step) & (NX - 1)], column_x.at[step, 0],
               cx_send.at[0], cx_recv.at[0], at_x(step)).start()
    column_x[0, 0] = column_x[NX, x]
    settle(column_x.at[1:NX, 0], cx_recv.at[0])
    total = column_x[0, 0]
    for part in range(1, NX):
        total = total + column_x[part, 0]
    column_total_ref[...] = total

    settle(rows.at[0, 0:3], x_send.at[0])
    settle(rows.at[0:7], y_send.at[0])
    for half in (0, 1):
        settle(hats.at[half], u_send.at[half])
    settle(masses.at[0], u_send.at[2])
    settle(row_parts.at[0:LINE - 1], r_send.at[0])
    settle(column_y.at[1:NY], cy_send.at[0])
    settle(column_x.at[1:NX, 0], cx_send.at[0])


def on_device(users, items, item_scale, user_mass, item_mass):
    user_count = users.shape[0] * lax.axis_size("wide")
    item_count = items.shape[0] * lax.axis_size("wide") * lax.axis_size("narrow")
    dma = pltpu.SemaphoreType.DMA
    vmem = pl.BlockSpec(memory_space=pltpu.VMEM)
    row_total, column_total = pl.pallas_call(
        functools.partial(body, item_count),
        out_shape=(
            jax.ShapeDtypeStruct((8, 128), F32),
            jax.ShapeDtypeStruct((1, 128), F32),
        ),
        in_specs=[pl.BlockSpec(memory_space=pl.ANY)] * 4,
        out_specs=(vmem, vmem),
        scratch_shapes=[
            pltpu.VMEM((USERS, WIDTH), BF16),
            pltpu.VMEM((BLOCK, WIDTH), BF16),
            pltpu.VMEM((1, BLOCK), BF16),
            pltpu.VMEM((NY, NX, BLOCK + 16, WIDTH), BF16),
            pltpu.VMEM((TILES, WIDTH, TILE), BF16),
            pltpu.VMEM((TILES, 2 * WIDTH, TILE), BF16),
            pltpu.VMEM((NY, TILES, NX * BLOCK, TILE), BF16),
            pltpu.VMEM((TILES, 8, TILE), F32),
            pltpu.VMEM((LINE, 16, 128), F32),
            pltpu.VMEM((2, 8, 128), F32),
            pltpu.VMEM((16, 2 * USERS), BF16),
            pltpu.VMEM((NY, NX, 1, BLOCK), F32),
            pltpu.VMEM((NY, NX, 1, BLOCK), F32),
            pltpu.VMEM((NX + 1, NX, 1, BLOCK), F32),
            pltpu.VMEM((2, 8, 128), F32),
            dma((4,)),
            dma((1,)), dma((1,)),
            dma((1,)), dma((2, 5, 2)),
            dma((3,)), dma((3,)),
            dma((1,)), dma((1,)),
            dma((1,)), dma((1,)),
            dma((1,)), dma((1,)),
        ],
        compiler_params=pltpu.CompilerParams(
            collective_id=0, has_side_effects=True, vmem_limit_bytes=56 * 1024 * 1024
        ),
        cost_estimate=pl.CostEstimate(
            flops=2 * 4096 * 2048 * 256, bytes_accessed=1 << 20, transcendentals=4096 * 2048
        ),
        name="scaling",
    )(users, items, item_scale.reshape(1, 128), user_mass.reshape(8, 128))
    user_scale = user_mass / (row_total.reshape(1024) / item_count)
    item_scale_new = item_mass / (column_total.reshape(128) / user_count)
    return user_scale, item_scale_new


def solution(mesh):
    in_specs = (
        P("wide", None),
        P(("wide", "narrow"), None),
        P(("wide", "narrow")),
        P("wide"),
        P(("wide", "narrow")),
    )
    out_specs = (P("wide"), P(("wide", "narrow")))
    return jax.shard_map(
        on_device, mesh=mesh, in_specs=in_specs, out_specs=out_specs, check_vma=False
    )
```

```python
import functools
import math

import jax
import jax.numpy as jnp
from jax import lax
from jax.experimental import pallas as pl
from jax.experimental.pallas import tpu as pltpu
from jax.sharding import PartitionSpec as P

MESH = pl.DeviceIdType.MESH
F32 = jnp.float32
BF16 = jnp.bfloat16

NX, NY, NZ = 4, 8, 8
LINE = 2 * NZ
BLOCK = 128
HALF = 64
USERS = 1024
TILE = 512
TILES = 2 * USERS // TILE
PARTS = TILE // 128
WIDTH = 128
SCALE = 2.0 * math.log2(math.e)


def unit_rows(values, axis):
    squares = jnp.sum(values * values, axis=axis, keepdims=True) + 1e-06
    return (values * lax.rsqrt(squares)).astype(BF16)


def three_pieces(weight):
    value = 0.5 * jnp.log(weight)
    high = value.astype(BF16).astype(F32)
    middle = (value - high).astype(BF16).astype(F32)
    return high, middle, value - high - middle


def body(
    item_count,
    users_hbm, items_hbm, weight_hbm, mass_hbm,
    row_total_ref, column_total_ref,
    users_in, items_in, weight_in, rows, turned, users, kernel, row_acc, row_parts, masses,
    user_rows, column_send, column_y, column_x, column_half,
    in_sem, x_send, x_recv, y_send, y_recv, u_send, u_recv, r_send, r_recv,
    cy_send, cy_recv, cx_send, cx_recv,
):
    wide = lax.axis_index("wide")
    narrow = lax.axis_index("narrow")
    y = wide & (NY - 1)
    x = (wide >> 3) & (NX - 1)
    z_lo = wide >> 5
    line = ((narrow >> 1) << 2) | (z_lo << 1) | (narrow & 1)
    wide_no_y = wide - y
    wide_no_x = wide - (x << 3)
    wide_no_z = wide & (NX * NY - 1)

    def at_x(step):
        return (wide_no_x + (((x + step) & (NX - 1)) << 3), narrow)

    def at_y(step):
        return (wide_no_y + ((y + step) & (NY - 1)), narrow)

    def at_line(step):
        other = (line + step) & (LINE - 1)
        return (wide_no_z + (((other >> 1) & 1) << 5), ((other >> 2) << 1) | (other & 1))

    barrier = pltpu.get_barrier_semaphore()

    def greet(partner):
        pl.semaphore_signal(barrier, inc=1, device_id=partner, device_id_type=MESH)

    def greet_line(step, carry):
        greet(at_line(step))
        return carry

    for step in (1, 3, 2):
        greet(at_x(step))
    for step in (1, 7, 2, 6, 3, 5, 4):
        greet(at_y(step))
    lax.fori_loop(1, LINE, greet_line, 0)

    get_items = pltpu.make_async_copy(items_hbm, items_in, in_sem.at[0])
    get_weight = pltpu.make_async_copy(weight_hbm, weight_in, in_sem.at[1])
    get_users = pltpu.make_async_copy(users_hbm, users_in, in_sem.at[2])
    get_mass = pltpu.make_async_copy(mass_hbm, masses.at[z_lo], in_sem.at[3])
    get_items.start()
    get_weight.start()
    get_users.start()
    get_mass.start()

    get_items.wait()
    get_weight.wait()
    rows[0, x, 0:BLOCK, :] = unit_rows(items_in[...].astype(F32), 1)
    rows[0, x, BLOCK:BLOCK + 16, :] = jnp.broadcast_to(
        weight_in[...].astype(F32), (16, BLOCK)
    ).astype(BF16)

    pl.semaphore_wait(barrier, NX - 1 + NY - 1 + LINE - 1)

    def remote(src, dst, send, recv, partner):
        return pltpu.make_async_remote_copy(
            src_ref=src, dst_ref=dst, send_sem=send, recv_sem=recv,
            device_id=partner, device_id_type=MESH,
        )

    def settle(part, sem):
        pltpu.make_async_copy(part, part, sem).wait()

    for step in (1, 3, 2):
        remote(rows.at[0, x], rows.at[0, x], x_send.at[0], x_recv.at[0], at_x(step)).start()

    up, down = at_line(2), at_line(LINE - 2)
    get_users.wait()
    get_mass.wait()
    for half, partner in ((0, up), (1, down)):
        values = users_in[half * TILE:(half + 1) * TILE, :].astype(F32).T
        tile = z_lo * 2 + half
        users[tile, 0:WIDTH, :] = unit_rows(values, 0)
        part = users.at[tile, 0:WIDTH, :]
        remote(part, part, u_send.at[half], u_recv.at[half], partner).start()
    remote(masses.at[z_lo], masses.at[z_lo], u_send.at[2], u_recv.at[2], up).start()

    settle(rows.at[0, 0:3], x_recv.at[0])

    def slot_of(way, hop):
        return 7 if hop == 4 else max(2 * hop - 1 + way, 0) if hop else 0

    def y_copy(way, hop, half):
        pair = slice(2 * half, 2 * half + 2)
        return remote(
            rows.at[slot_of(way, hop - 1), pair], rows.at[slot_of(way, hop), pair],
            y_send.at[0], y_recv.at[way, hop, half], at_y(NY - 1 if way else 1),
        )

    for half in (0, 1):
        for way in (0, 1):
            y_copy(way, 1, half).start()

    ones = jnp.ones((WIDTH, TILE), BF16)
    for tile in range(TILES):
        users[tile, WIDTH:2 * WIDTH, :] = ones
    row_acc[...] = jnp.zeros_like(row_acc)

    sub = lax.broadcasted_iota(jnp.int32, (8, BLOCK), 0)

    def turn(slot):
        value = jnp.ones((8, BLOCK), F32)
        for block in range(NX):
            weight = rows[slot, block, BLOCK:BLOCK + 16, :].astype(F32)[0:8]
            value = jnp.where((sub & 3) == block, weight, value)
        high, middle, low = three_pieces(value)
        first = jnp.where(sub < 4, high, middle)
        second = jnp.where(sub < 4, low, 0.0)
        stacked = jnp.concatenate([first, second, jnp.zeros((BLOCK - 16, BLOCK), F32)], axis=0)
        turned[...] = stacked.T.astype(BF16)

    lane = lax.broadcasted_iota(jnp.int32, (1, BLOCK), 1)

    pieces = [(hop, way, half) for hop in (1, 2, 3) for way in (0, 1) for half in (0, 1)]
    pieces += [(4, 0, 0), (4, 1, 1)]

    def pass_on(hop, way, half):
        y_copy(way, hop, half).wait_recv()
        if hop < 3 or (hop == 3 and half == way):
            y_copy(way, hop + 1, half).start()

    def compute_step(at, carry):
        slot, later = at >> 1, at & 1
        for known, piece in enumerate(pieces):
            @pl.when(at == known)
            def _():
                pass_on(*piece)

        @pl.when(later == 0)
        def _():
            turn(slot)

        @pl.when(at == 1)
        def _():
            for half in (0, 1):
                settle(users.at[half, 0:WIDTH, :], u_recv.at[half])
            settle(masses.at[0], u_recv.at[2])

        block_of_users = (z_lo + later) & 1
        accs = [jnp.zeros((8, TILE), F32) for _ in range(2)]
        bias = turned[...]
        for block in range(NX):
            kept = ((lane & 3) == block).astype(F32).astype(BF16)
            left = jnp.concatenate([rows[slot, block, 0:BLOCK, :], bias * kept], axis=1)
            for part in range(2):
                tile = block_of_users * 2 + part
                scores = jnp.dot(left, users[tile], preferred_element_type=F32)
                values = jnp.exp2((scores * SCALE).astype(BF16))
                kernel[slot, tile, block * BLOCK:(block + 1) * BLOCK] = values
                accs[part] += jnp.sum(values.astype(F32).reshape(BLOCK // 8, 8, TILE), axis=0)
        for part in range(2):
            row_acc[block_of_users * 2 + part] += accs[part]
        return carry

    lax.fori_loop(0, 16, compute_step, 0)

    for tile in range(TILES):
        total = jnp.sum(row_acc[tile], axis=0, keepdims=True)
        for part in range(PARTS):
            at = tile * PARTS + part
            row_parts[line, at:at + 1, :] = total[:, part * 128:(part + 1) * 128]

    def send_rows(step, carry):
        remote(row_parts.at[line], row_parts.at[line], r_send.at[0], r_recv.at[0],
               at_line(step)).start()
        return carry

    lax.fori_loop(1, LINE, send_rows, 0)
    settle(row_parts.at[0:LINE - 1], r_recv.at[0])
    total = row_parts[0]
    for part in range(1, LINE):
        total = total + row_parts[part]
    scale = masses[...].reshape(16, 128) / (total / item_count)
    for at in range(TILES * PARTS):
        user_rows[at] = jnp.broadcast_to(scale[at:at + 1, :], (8, 128))
    column_half[...] = total.reshape(2, 8, 128)
    row_total_ref[...] = column_half[z_lo]

    def sum_columns(slot):
        for block in range(NX):
            pieces = []
            for half in (0, 1):
                acc = jnp.zeros((HALF // 8, 8, 128), F32)
                for tile in range(TILES):
                    for part in range(PARTS):
                        piece = kernel[slot, tile,
                                       block * BLOCK + half * HALF:block * BLOCK + (half + 1) * HALF,
                                       part * 128:(part + 1) * 128]
                        piece = piece.astype(F32).reshape(HALF // 8, 8, 128)
                        acc = acc + piece * user_rows[tile * PARTS + part]
                pieces.append(acc.reshape(HALF, 128))
            flat = jnp.concatenate(pieces, axis=0).T
            column_send[slot, block] = jnp.sum(flat, axis=0, keepdims=True)

    def column_step(step, carry):
        slot = step & (NY - 1)
        sum_columns(slot)
        hop = (step + 1) >> 1
        ahead = jnp.where((step & 1) == 0, hop, NY - hop)

        @pl.when(step < NY)
        def _():
            remote(column_send.at[slot], column_y.at[slot], cy_send.at[0], cy_recv.at[0],
                   at_y(ahead)).start()

        return carry

    lax.fori_loop(1, NY + 1, column_step, 0)
    column_y[0] = column_send[0]
    settle(column_y.at[1:NY], cy_recv.at[0])
    total = column_y[0]
    for part in range(1, NY):
        total = total + column_y[part]
    column_x[NX] = total

    for step in (1, 3, 2):
        remote(column_x.at[NX, (x + step) & (NX - 1)], column_x.at[step, 0],
               cx_send.at[0], cx_recv.at[0], at_x(step)).start()
    column_x[0, 0] = column_x[NX, x]
    settle(column_x.at[1:NX, 0], cx_recv.at[0])
    total = column_x[0, 0]
    for part in range(1, NX):
        total = total + column_x[part, 0]
    weight = weight_in[...].astype(F32)
    column_total_ref[...] = total / weight

    settle(rows.at[0, 0:3], x_send.at[0])
    settle(rows.at[0:7], y_send.at[0])
    for half in (0, 1):
        settle(users.at[half, 0:WIDTH, :], u_send.at[half])
    settle(masses.at[0], u_send.at[2])
    settle(row_parts.at[0:LINE - 1], r_send.at[0])
    settle(column_y.at[1:NY], cy_send.at[0])
    settle(column_x.at[1:NX, 0], cx_send.at[0])


def on_device(users, items, item_scale, user_mass, item_mass):
    user_count = users.shape[0] * lax.axis_size("wide")
    item_count = items.shape[0] * lax.axis_size("wide") * lax.axis_size("narrow")
    dma = pltpu.SemaphoreType.DMA
    vmem = pl.BlockSpec(memory_space=pltpu.VMEM)
    row_total, column_total = pl.pallas_call(
        functools.partial(body, item_count),
        out_shape=(
            jax.ShapeDtypeStruct((8, 128), F32),
            jax.ShapeDtypeStruct((1, 128), F32),
        ),
        in_specs=[pl.BlockSpec(memory_space=pl.ANY)] * 4,
        out_specs=(vmem, vmem),
        scratch_shapes=[
            pltpu.VMEM((USERS, WIDTH), BF16),
            pltpu.VMEM((BLOCK, WIDTH), BF16),
            pltpu.VMEM((1, BLOCK), BF16),
            pltpu.VMEM((NY, NX, BLOCK + 16, WIDTH), BF16),
            pltpu.VMEM((BLOCK, BLOCK), BF16),
            pltpu.VMEM((TILES, 2 * WIDTH, TILE), BF16),
            pltpu.VMEM((NY, TILES, NX * BLOCK, TILE), BF16),
            pltpu.VMEM((TILES, 8, TILE), F32),
            pltpu.VMEM((LINE, 16, 128), F32),
            pltpu.VMEM((2, 8, 128), F32),
            pltpu.VMEM((TILES * PARTS, 8, 128), F32),
            pltpu.VMEM((NY, NX, 1, BLOCK), F32),
            pltpu.VMEM((NY, NX, 1, BLOCK), F32),
            pltpu.VMEM((NX + 1, NX, 1, BLOCK), F32),
            pltpu.VMEM((2, 8, 128), F32),
            dma((4,)),
            dma((1,)), dma((1,)),
            dma((1,)), dma((2, 5, 2)),
            dma((3,)), dma((3,)),
            dma((1,)), dma((1,)),
            dma((1,)), dma((1,)),
            dma((1,)), dma((1,)),
        ],
        compiler_params=pltpu.CompilerParams(
            collective_id=0, has_side_effects=True, vmem_limit_bytes=56 * 1024 * 1024
        ),
        cost_estimate=pl.CostEstimate(
            flops=2 * 4096 * 2048 * 256, bytes_accessed=1 << 20, transcendentals=4096 * 2048
        ),
        name="scaling",
    )(users, items, item_scale.reshape(1, 128), user_mass.reshape(8, 128))
    user_scale = user_mass / (row_total.reshape(1024) / item_count)
    item_scale_new = item_mass / (column_total.reshape(128) / user_count)
    return user_scale, item_scale_new


def solution(mesh):
    in_specs = (
        P("wide", None),
        P(("wide", "narrow"), None),
        P(("wide", "narrow")),
        P("wide"),
        P(("wide", "narrow")),
    )
    out_specs = (P("wide"), P(("wide", "narrow")))
    return jax.shard_map(
        on_device, mesh=mesh, in_specs=in_specs, out_specs=out_specs, check_vma=False
    )
```

```python
import functools
import math

import jax
import jax.numpy as jnp
from jax import lax
from jax.experimental import pallas as pl
from jax.experimental.pallas import tpu as pltpu
from jax.sharding import PartitionSpec as P

MESH = pl.DeviceIdType.MESH
F32 = jnp.float32
BF16 = jnp.bfloat16

NX, NY, NZ = 4, 8, 8
LINE = 2 * NZ
BLOCK = 128
HALF = 64
USERS = 1024
TILE = 512
TILES = 2 * USERS // TILE
PARTS = TILE // 128
WIDTH = 128
SCALE = 2.0 * math.log2(math.e)


def unit_rows(values, axis):
    squares = jnp.sum(values * values, axis=axis, keepdims=True) + 1e-06
    return (values * lax.rsqrt(squares)).astype(BF16)


def body(
    item_count,
    users_hbm, items_hbm, weight_hbm, mass_hbm,
    row_total_ref, column_total_ref,
    users_in, items_in, weight_in, rows, spread, users, kernel, row_acc, row_parts, masses,
    user_rows, column_send, column_y, column_x, column_half,
    in_sem, x_send, x_recv, y_send, y_recv, u_send, u_recv, r_send, r_recv,
    cy_send, cy_recv, cx_send, cx_recv,
):
    wide = lax.axis_index("wide")
    narrow = lax.axis_index("narrow")
    y = wide & (NY - 1)
    x = (wide >> 3) & (NX - 1)
    z_lo = wide >> 5
    line = ((narrow >> 1) << 2) | (z_lo << 1) | (narrow & 1)
    wide_no_y = wide - y
    wide_no_x = wide - (x << 3)
    wide_no_z = wide & (NX * NY - 1)

    def at_x(step):
        return (wide_no_x + (((x + step) & (NX - 1)) << 3), narrow)

    def at_y(step):
        return (wide_no_y + ((y + step) & (NY - 1)), narrow)

    def at_line(step):
        other = (line + step) & (LINE - 1)
        return (wide_no_z + (((other >> 1) & 1) << 5), ((other >> 2) << 1) | (other & 1))

    barrier = pltpu.get_barrier_semaphore()

    def greet(partner):
        pl.semaphore_signal(barrier, inc=1, device_id=partner, device_id_type=MESH)

    def greet_line(step, carry):
        greet(at_line(step))
        return carry

    for step in (1, 3, 2):
        greet(at_x(step))
    for step in (1, 7, 2, 6, 3, 5, 4):
        greet(at_y(step))
    lax.fori_loop(1, LINE, greet_line, 0)

    get_items = pltpu.make_async_copy(items_hbm, items_in, in_sem.at[0])
    get_weight = pltpu.make_async_copy(weight_hbm, weight_in, in_sem.at[1])
    get_users = pltpu.make_async_copy(users_hbm, users_in, in_sem.at[2])
    get_mass = pltpu.make_async_copy(mass_hbm, masses.at[z_lo], in_sem.at[3])
    get_items.start()
    get_weight.start()
    get_users.start()
    get_mass.start()

    get_items.wait()
    get_weight.wait()
    rows[0, x, 0:BLOCK, :] = unit_rows(items_in[...].astype(F32), 1)
    rows[0, x, BLOCK:BLOCK + 16, :] = jnp.broadcast_to(
        weight_in[...].astype(F32), (16, BLOCK)
    ).astype(BF16)

    pl.semaphore_wait(barrier, NX - 1 + NY - 1 + LINE - 1)

    def remote(src, dst, send, recv, partner):
        return pltpu.make_async_remote_copy(
            src_ref=src, dst_ref=dst, send_sem=send, recv_sem=recv,
            device_id=partner, device_id_type=MESH,
        )

    def settle(part, sem):
        pltpu.make_async_copy(part, part, sem).wait()

    for step in (1, 3, 2):
        remote(rows.at[0, x], rows.at[0, x], x_send.at[0], x_recv.at[0], at_x(step)).start()

    up, down = at_line(2), at_line(LINE - 2)
    get_users.wait()
    get_mass.wait()
    for half, partner in ((0, up), (1, down)):
        values = users_in[half * TILE:(half + 1) * TILE, :].astype(F32).T
        tile = z_lo * 2 + half
        users[tile] = unit_rows(values, 0)
        part = users.at[tile]
        remote(part, part, u_send.at[half], u_recv.at[half], partner).start()
    remote(masses.at[z_lo], masses.at[z_lo], u_send.at[2], u_recv.at[2], up).start()

    settle(rows.at[0, 0:3], x_recv.at[0])

    def slot_of(way, hop):
        return 7 if hop == 4 else max(2 * hop - 1 + way, 0) if hop else 0

    def y_copy(way, hop, half):
        pair = slice(2 * half, 2 * half + 2)
        return remote(
            rows.at[slot_of(way, hop - 1), pair], rows.at[slot_of(way, hop), pair],
            y_send.at[0], y_recv.at[way, hop, half], at_y(NY - 1 if way else 1),
        )

    for half in (0, 1):
        for way in (0, 1):
            y_copy(way, 1, half).start()

    row_acc[...] = jnp.zeros_like(row_acc)

    def spread_weights(slot):
        for block in range(NX):
            weight = rows[slot, block, BLOCK:BLOCK + 16, :].astype(F32)[0:1]
            spread[slot, block * BLOCK:(block + 1) * BLOCK] = jnp.broadcast_to(
                weight, (BLOCK, BLOCK)
            ).T

    def before(hop):
        if hop == 0:
            spread_weights(0)
            return
        for half in (0, 1):
            for way in (0, 1):
                if hop < 4 or half == way:
                    y_copy(way, hop, half).wait_recv()
                if hop < 3 or (hop == 3 and half == way):
                    y_copy(way, hop + 1, half).start()
        for slot in sorted({slot_of(0, hop), slot_of(1, hop)}):
            spread_weights(slot)

    def compute_step(at, carry):
        slot, later = at >> 1, at & 1
        for known, hop in ((0, 0), (2, 1), (6, 2), (10, 3), (14, 4)):
            @pl.when(at == known)
            def _():
                before(hop)

        @pl.when(at == 1)
        def _():
            for half in (0, 1):
                settle(users.at[half], u_recv.at[half])
            settle(masses.at[0], u_recv.at[2])

        block_of_users = (z_lo + later) & 1
        accs = [jnp.zeros((8, TILE), F32) for _ in range(2)]
        for pair in range(NX // 2):
            left = jnp.concatenate(
                [rows[slot, block, 0:BLOCK, :] for block in (2 * pair, 2 * pair + 1)], axis=0
            )
            here = slice(pair * 2 * BLOCK, (pair + 1) * 2 * BLOCK)
            weight = jnp.concatenate([spread[slot, here]] * PARTS, axis=1)
            for part in range(2):
                tile = block_of_users * 2 + part
                scores = jnp.dot(left, users[tile], preferred_element_type=F32)
                values = jnp.exp2((scores * SCALE).astype(BF16))
                kernel[slot, tile, here] = values
                weighted = values.astype(F32) * weight
                accs[part] += jnp.sum(weighted.reshape(2 * BLOCK // 8, 8, TILE), axis=0)
        for part in range(2):
            row_acc[block_of_users * 2 + part] += accs[part]
        return carry

    lax.fori_loop(0, 16, compute_step, 0)

    for tile in range(TILES):
        total = jnp.sum(row_acc[tile], axis=0, keepdims=True)
        for part in range(PARTS):
            at = tile * PARTS + part
            row_parts[line, at:at + 1, :] = total[:, part * 128:(part + 1) * 128]

    def send_rows(step, carry):
        remote(row_parts.at[line], row_parts.at[line], r_send.at[0], r_recv.at[0],
               at_line(step)).start()
        return carry

    lax.fori_loop(1, LINE, send_rows, 0)
    settle(row_parts.at[0:LINE - 1], r_recv.at[0])
    total = row_parts[0]
    for part in range(1, LINE):
        total = total + row_parts[part]
    scale = masses[...].reshape(16, 128) / (total / item_count)
    for at in range(TILES * PARTS):
        user_rows[at] = jnp.broadcast_to(scale[at:at + 1, :], (8, 128))
    column_half[...] = total.reshape(2, 8, 128)
    row_total_ref[...] = column_half[z_lo]

    def sum_columns(slot):
        for block in range(NX):
            pieces = []
            for half in (0, 1):
                acc = jnp.zeros((HALF // 8, 8, 128), F32)
                for tile in range(TILES):
                    for part in range(PARTS):
                        piece = kernel[slot, tile,
                                       block * BLOCK + half * HALF:block * BLOCK + (half + 1) * HALF,
                                       part * 128:(part + 1) * 128]
                        piece = piece.astype(F32).reshape(HALF // 8, 8, 128)
                        acc = acc + piece * user_rows[tile * PARTS + part]
                pieces.append(acc.reshape(HALF, 128))
            flat = jnp.concatenate(pieces, axis=0).T
            column_send[slot, block] = jnp.sum(flat, axis=0, keepdims=True)

    def column_step(step, carry):
        slot = step & (NY - 1)
        sum_columns(slot)
        hop = (step + 1) >> 1
        ahead = jnp.where((step & 1) == 0, hop, NY - hop)

        @pl.when(step < NY)
        def _():
            remote(column_send.at[slot], column_y.at[slot], cy_send.at[0], cy_recv.at[0],
                   at_y(ahead)).start()

        return carry

    lax.fori_loop(1, NY + 1, column_step, 0)
    column_y[0] = column_send[0]
    settle(column_y.at[1:NY], cy_recv.at[0])
    total = column_y[0]
    for part in range(1, NY):
        total = total + column_y[part]
    column_x[NX] = total

    for step in (1, 3, 2):
        remote(column_x.at[NX, (x + step) & (NX - 1)], column_x.at[step, 0],
               cx_send.at[0], cx_recv.at[0], at_x(step)).start()
    column_x[0, 0] = column_x[NX, x]
    settle(column_x.at[1:NX, 0], cx_recv.at[0])
    total = column_x[0, 0]
    for part in range(1, NX):
        total = total + column_x[part, 0]
    column_total_ref[...] = total

    settle(rows.at[0, 0:3], x_send.at[0])
    settle(rows.at[0:7], y_send.at[0])
    for half in (0, 1):
        settle(users.at[half], u_send.at[half])
    settle(masses.at[0], u_send.at[2])
    settle(row_parts.at[0:LINE - 1], r_send.at[0])
    settle(column_y.at[1:NY], cy_send.at[0])
    settle(column_x.at[1:NX, 0], cx_send.at[0])


def on_device(users, items, item_scale, user_mass, item_mass):
    user_count = users.shape[0] * lax.axis_size("wide")
    item_count = items.shape[0] * lax.axis_size("wide") * lax.axis_size("narrow")
    dma = pltpu.SemaphoreType.DMA
    vmem = pl.BlockSpec(memory_space=pltpu.VMEM)
    row_total, column_total = pl.pallas_call(
        functools.partial(body, item_count),
        out_shape=(
            jax.ShapeDtypeStruct((8, 128), F32),
            jax.ShapeDtypeStruct((1, 128), F32),
        ),
        in_specs=[pl.BlockSpec(memory_space=pl.ANY)] * 4,
        out_specs=(vmem, vmem),
        scratch_shapes=[
            pltpu.VMEM((USERS, WIDTH), BF16),
            pltpu.VMEM((BLOCK, WIDTH), BF16),
            pltpu.VMEM((1, BLOCK), BF16),
            pltpu.VMEM((NY, NX, BLOCK + 16, WIDTH), BF16),
            pltpu.VMEM((NY, NX * BLOCK, BLOCK), F32),
            pltpu.VMEM((TILES, WIDTH, TILE), BF16),
            pltpu.VMEM((NY, TILES, NX * BLOCK, TILE), BF16),
            pltpu.VMEM((TILES, 8, TILE), F32),
            pltpu.VMEM((LINE, 16, 128), F32),
            pltpu.VMEM((2, 8, 128), F32),
            pltpu.VMEM((TILES * PARTS, 8, 128), F32),
            pltpu.VMEM((NY, NX, 1, BLOCK), F32),
            pltpu.VMEM((NY, NX, 1, BLOCK), F32),
            pltpu.VMEM((NX + 1, NX, 1, BLOCK), F32),
            pltpu.VMEM((2, 8, 128), F32),
            dma((4,)),
            dma((1,)), dma((1,)),
            dma((1,)), dma((2, 5, 2)),
            dma((3,)), dma((3,)),
            dma((1,)), dma((1,)),
            dma((1,)), dma((1,)),
            dma((1,)), dma((1,)),
        ],
        compiler_params=pltpu.CompilerParams(
            collective_id=0, has_side_effects=True, vmem_limit_bytes=56 * 1024 * 1024
        ),
        cost_estimate=pl.CostEstimate(
            flops=2 * 4096 * 2048 * 256, bytes_accessed=1 << 20, transcendentals=4096 * 2048
        ),
        name="scaling",
    )(users, items, item_scale.reshape(1, 128), user_mass.reshape(8, 128))
    user_scale = user_mass / (row_total.reshape(1024) / item_count)
    item_scale_new = item_mass / (column_total.reshape(128) / user_count)
    return user_scale, item_scale_new


def solution(mesh):
    in_specs = (
        P("wide", None),
        P(("wide", "narrow"), None),
        P(("wide", "narrow")),
        P("wide"),
        P(("wide", "narrow")),
    )
    out_specs = (P("wide"), P(("wide", "narrow")))
    return jax.shard_map(
        on_device, mesh=mesh, in_specs=in_specs, out_specs=out_specs, check_vma=False
    )
```

```python
import functools
import math

import jax
import jax.numpy as jnp
from jax import lax
from jax.experimental import pallas as pl
from jax.experimental.pallas import tpu as pltpu
from jax.sharding import PartitionSpec as P

MESH = pl.DeviceIdType.MESH
F32 = jnp.float32
BF16 = jnp.bfloat16

NX, NY, NZ = 4, 8, 8
LINE = 2 * NZ
BLOCK = 128
HALF = 64
USERS = 1024
TILE = 512
TILES = 2 * USERS // TILE
PARTS = TILE // 128
WIDTH = 128
SCALE = 2.0 * math.log2(math.e)


def unit_rows(values, axis):
    squares = jnp.sum(values * values, axis=axis, keepdims=True) + 1e-06
    return (values * lax.rsqrt(squares)).astype(BF16)


def body(
    item_count,
    users_hbm, items_hbm, weight_hbm, mass_hbm,
    row_total_ref, column_total_ref,
    users_in, items_in, weight_in, rows, spread, users, kernel, row_acc, row_parts, masses,
    user_rows, column_send, column_y, column_x, column_half,
    in_sem, x_send, x_recv, y_send, y_recv, f_recv, u_send, u_recv, r_send, r_recv,
    cy_send, cy_recv, cx_send, cx_recv,
):
    wide = lax.axis_index("wide")
    narrow = lax.axis_index("narrow")
    y = wide & (NY - 1)
    x = (wide >> 3) & (NX - 1)
    z_lo = wide >> 5
    line = ((narrow >> 1) << 2) | (z_lo << 1) | (narrow & 1)
    wide_no_y = wide - y
    wide_no_x = wide - (x << 3)
    wide_no_z = wide & (NX * NY - 1)

    def at_x(step):
        return (wide_no_x + (((x + step) & (NX - 1)) << 3), narrow)

    def at_y(step):
        return (wide_no_y + ((y + step) & (NY - 1)), narrow)

    def at_line(step):
        other = (line + step) & (LINE - 1)
        return (wide_no_z + (((other >> 1) & 1) << 5), ((other >> 2) << 1) | (other & 1))

    barrier = pltpu.get_barrier_semaphore()

    def greet(partner):
        pl.semaphore_signal(barrier, inc=1, device_id=partner, device_id_type=MESH)

    def greet_line(step, carry):
        greet(at_line(step))
        return carry

    for step in (1, 3, 2):
        greet(at_x(step))
    for step in (1, 7, 2, 6, 3, 5, 4):
        greet(at_y(step))
    lax.fori_loop(1, LINE, greet_line, 0)

    get_items = pltpu.make_async_copy(items_hbm, items_in, in_sem.at[0])
    get_weight = pltpu.make_async_copy(weight_hbm, weight_in, in_sem.at[1])
    get_users = pltpu.make_async_copy(users_hbm, users_in, in_sem.at[2])
    get_mass = pltpu.make_async_copy(mass_hbm, masses.at[z_lo], in_sem.at[3])
    get_items.start()
    get_weight.start()
    get_users.start()
    get_mass.start()

    get_items.wait()
    get_weight.wait()
    rows[0, 0, 0:BLOCK, :] = unit_rows(items_in[...].astype(F32), 1)
    rows[0, 0, BLOCK:BLOCK + 16, :] = jnp.broadcast_to(
        weight_in[...].astype(F32), (16, BLOCK)
    ).astype(BF16)

    pl.semaphore_wait(barrier, NX - 1 + NY - 1 + LINE - 1)

    def remote(src, dst, send, recv, partner):
        return pltpu.make_async_remote_copy(
            src_ref=src, dst_ref=dst, send_sem=send, recv_sem=recv,
            device_id=partner, device_id_type=MESH,
        )

    def settle(part, sem):
        pltpu.make_async_copy(part, part, sem).wait()

    own = rows.at[0, 0]
    left, right, far = at_x(3), at_x(1), at_x(2)

    def y_send_to(hop):
        if hop == 4:
            remote(own, rows.at[0, 7], y_send.at[0], y_recv.at[4], at_y(4)).start()
            return
        remote(own, rows.at[0, 2 * hop - 1], y_send.at[0], y_recv.at[hop], at_y(hop)).start()
        remote(own, rows.at[0, 2 * hop], y_send.at[0], y_recv.at[hop], at_y(NY - hop)).start()

    def slots_of(hop):
        return slice(2 * hop - 1, 2 * hop + 1) if 0 < hop < 4 else slice(7, 8) if hop else slice(0, 1)

    def x_send_of(hop):
        part = rows.at[0, slots_of(hop)]
        remote(part, rows.at[1, slots_of(hop)], x_send.at[0], x_recv.at[hop], right).start()
        remote(part, rows.at[2, slots_of(hop)], x_send.at[0], x_recv.at[hop], left).start()
        if hop in (0, 4):
            remote(part, rows.at[3, slots_of(hop)], x_send.at[0], x_recv.at[hop], far).start()

    def from_y(hop):
        settle(rows.at[0, slots_of(hop)], y_recv.at[hop])
        x_send_of(hop)

    def from_x(hop):
        if hop in (0, 4):
            settle(rows.at[1:4, slots_of(hop)], x_recv.at[hop])
            return
        settle(rows.at[1:3, slots_of(hop)], x_recv.at[hop])
        behind, ahead = 2 * hop - 1, 2 * hop
        remote(rows.at[1, behind], rows.at[3, behind], x_send.at[0], f_recv.at[hop], right).start()
        remote(rows.at[2, ahead], rows.at[3, ahead], x_send.at[0], f_recv.at[hop], left).start()

    def from_far(hop):
        settle(rows.at[3, slots_of(hop)], f_recv.at[hop])

    y_send_to(1)
    x_send_of(0)
    y_send_to(2)
    y_send_to(3)
    y_send_to(4)

    up, down = at_line(2), at_line(LINE - 2)
    get_users.wait()
    get_mass.wait()
    for half, partner in ((0, up), (1, down)):
        values = users_in[half * TILE:(half + 1) * TILE, :].astype(F32).T
        tile = z_lo * 2 + half
        users[tile] = unit_rows(values, 0)
        part = users.at[tile]
        remote(part, part, u_send.at[half], u_recv.at[half], partner).start()
    remote(masses.at[z_lo], masses.at[z_lo], u_send.at[2], u_recv.at[2], up).start()

    from_y(1)
    from_y(2)
    row_acc[...] = jnp.zeros_like(row_acc)

    def unit_of(unit):
        late = jnp.logical_or(unit == 3, unit >= 5)
        column = jnp.where(unit < 3, unit, jnp.where(unit == 3, 0, jnp.where(unit == 4, 3, unit - 4)))
        return column, jnp.where(late, 4, 0)

    def spread_weights(column, first):
        for block in range(4):
            weight = rows[column, first + block, BLOCK:BLOCK + 16, :].astype(F32)[0:1]
            spread[block * BLOCK:(block + 1) * BLOCK] = jnp.broadcast_to(weight, (BLOCK, BLOCK)).T

    def before(at):
        if at == 2:
            from_y(3)
            from_x(0)
            from_x(1)
            from_x(2)
        elif at == 5:
            from_y(4)
        elif at == 6:
            from_x(3)
        elif at == 8:
            from_far(1)
            from_far(2)
        elif at == 10:
            from_x(4)
        elif at == 14:
            from_far(3)

    def compute_step(at, carry):
        unit, later = at >> 1, at & 1
        column, first = unit_of(unit)
        for known in (2, 5, 6, 8, 10, 14):
            @pl.when(at == known)
            def _():
                before(known)

        @pl.when(later == 0)
        def _():
            spread_weights(column, first)

        @pl.when(at == 1)
        def _():
            for half in (0, 1):
                settle(users.at[half], u_recv.at[half])
            settle(masses.at[0], u_recv.at[2])

        block_of_users = (z_lo + later) & 1
        accs = [jnp.zeros((8, TILE), F32) for _ in range(2)]
        for pair in range(2):
            left = jnp.concatenate(
                [rows[column, first + 2 * pair + block, 0:BLOCK, :] for block in range(2)], axis=0
            )
            here = slice(pair * 2 * BLOCK, (pair + 1) * 2 * BLOCK)
            weight = jnp.concatenate([spread[here]] * PARTS, axis=1)
            for part in range(2):
                tile = block_of_users * 2 + part
                scores = jnp.dot(left, users[tile], preferred_element_type=F32)
                values = jnp.exp2((scores * SCALE).astype(BF16))
                kernel[unit, tile, here] = values
                weighted = values.astype(F32) * weight
                accs[part] += jnp.sum(weighted.reshape(2 * BLOCK // 8, 8, TILE), axis=0)
        for part in range(2):
            row_acc[block_of_users * 2 + part] += accs[part]
        return carry

    lax.fori_loop(0, 16, compute_step, 0)

    for tile in range(TILES):
        total = jnp.sum(row_acc[tile], axis=0, keepdims=True)
        for part in range(PARTS):
            at = tile * PARTS + part
            row_parts[line, at:at + 1, :] = total[:, part * 128:(part + 1) * 128]

    def send_rows(step, carry):
        remote(row_parts.at[line], row_parts.at[line], r_send.at[0], r_recv.at[0],
               at_line(step)).start()
        return carry

    lax.fori_loop(1, LINE, send_rows, 0)
    settle(row_parts.at[0:LINE - 1], r_recv.at[0])
    total = row_parts[0]
    for part in range(1, LINE):
        total = total + row_parts[part]
    scale = masses[...].reshape(16, 128) / (total / item_count)
    for at in range(TILES * PARTS):
        user_rows[at] = jnp.broadcast_to(scale[at:at + 1, :], (8, 128))
    column_half[...] = total.reshape(2, 8, 128)
    row_total_ref[...] = column_half[z_lo]

    def sum_columns(unit, column, first):
        for block in range(4):
            pieces = []
            for half in (0, 1):
                acc = jnp.zeros((HALF // 8, 8, 128), F32)
                for tile in range(TILES):
                    for part in range(PARTS):
                        piece = kernel[unit, tile,
                                       block * BLOCK + half * HALF:block * BLOCK + (half + 1) * HALF,
                                       part * 128:(part + 1) * 128]
                        piece = piece.astype(F32).reshape(HALF // 8, 8, 128)
                        acc = acc + piece * user_rows[tile * PARTS + part]
                pieces.append(acc.reshape(HALF, 128))
            flat = jnp.concatenate(pieces, axis=0).T
            column_send[first + block, column] = jnp.sum(flat, axis=0, keepdims=True)

    def send_columns(slot):
        hop = (slot + 1) // 2
        remote(column_send.at[slot], column_y.at[slot], cy_send.at[0], cy_recv.at[0],
               at_y(NY - hop if slot % 2 else hop)).start()

    def column_step(step, carry):
        column = step & 3
        late = step < 4
        unit = jnp.where(
            late, jnp.where(column == 0, 3, column + 4), jnp.where(column == 3, 4, column)
        )
        sum_columns(unit, column, jnp.where(late, 4, 0))

        @pl.when(step == 3)
        def _():
            for slot in (7, 5, 6, 4):
                send_columns(slot)

        return carry

    lax.fori_loop(0, 8, column_step, 0)
    for slot in (3, 1, 2):
        send_columns(slot)
    column_y[0] = column_send[0]
    settle(column_y.at[1:NY], cy_recv.at[0])
    total = column_y[0]
    for part in range(1, NY):
        total = total + column_y[part]
    column_x[NX] = total
    for column, source, partner in ((3, 3, far), (1, 2, left), (2, 1, right)):
        remote(column_x.at[NX, column], column_x.at[source, 0],
               cx_send.at[0], cx_recv.at[0], partner).start()
    column_x[0, 0] = column_x[NX, 0]
    settle(column_x.at[1:NX, 0], cx_recv.at[0])
    total = column_x[0, 0]
    for part in range(1, NX):
        total = total + column_x[part, 0]
    column_total_ref[...] = total

    settle(rows.at[0, 1:NY], y_send.at[0])
    settle(rows.at[1:NX], x_send.at[0])
    for half in (0, 1):
        settle(users.at[half], u_send.at[half])
    settle(masses.at[0], u_send.at[2])
    settle(row_parts.at[0:LINE - 1], r_send.at[0])
    settle(column_y.at[1:NY], cy_send.at[0])
    settle(column_x.at[1:NX, 0], cx_send.at[0])


def on_device(users, items, item_scale, user_mass, item_mass):
    user_count = users.shape[0] * lax.axis_size("wide")
    item_count = items.shape[0] * lax.axis_size("wide") * lax.axis_size("narrow")
    dma = pltpu.SemaphoreType.DMA
    vmem = pl.BlockSpec(memory_space=pltpu.VMEM)
    row_total, column_total = pl.pallas_call(
        functools.partial(body, item_count),
        out_shape=(
            jax.ShapeDtypeStruct((8, 128), F32),
            jax.ShapeDtypeStruct((1, 128), F32),
        ),
        in_specs=[pl.BlockSpec(memory_space=pl.ANY)] * 4,
        out_specs=(vmem, vmem),
        scratch_shapes=[
            pltpu.VMEM((USERS, WIDTH), BF16),
            pltpu.VMEM((BLOCK, WIDTH), BF16),
            pltpu.VMEM((1, BLOCK), BF16),
            pltpu.VMEM((NX, NY, BLOCK + 16, WIDTH), BF16),
            pltpu.VMEM((4 * BLOCK, BLOCK), F32),
            pltpu.VMEM((TILES, WIDTH, TILE), BF16),
            pltpu.VMEM((NY, TILES, 4 * BLOCK, TILE), BF16),
            pltpu.VMEM((TILES, 8, TILE), F32),
            pltpu.VMEM((LINE, 16, 128), F32),
            pltpu.VMEM((2, 8, 128), F32),
            pltpu.VMEM((TILES * PARTS, 8, 128), F32),
            pltpu.VMEM((NY, NX, 1, BLOCK), F32),
            pltpu.VMEM((NY, NX, 1, BLOCK), F32),
            pltpu.VMEM((NX + 1, NX, 1, BLOCK), F32),
            pltpu.VMEM((2, 8, 128), F32),
            dma((4,)),
            dma((1,)), dma((5,)),
            dma((1,)), dma((5,)),
            dma((4,)),
            dma((3,)), dma((3,)),
            dma((1,)), dma((1,)),
            dma((1,)), dma((1,)),
            dma((1,)), dma((1,)),
        ],
        compiler_params=pltpu.CompilerParams(
            collective_id=0, has_side_effects=True, vmem_limit_bytes=56 * 1024 * 1024
        ),
        cost_estimate=pl.CostEstimate(
            flops=2 * 4096 * 2048 * 256, bytes_accessed=1 << 20, transcendentals=4096 * 2048
        ),
        name="scaling",
    )(users, items, item_scale.reshape(1, 128), user_mass.reshape(8, 128))
    user_scale = user_mass / (row_total.reshape(1024) / item_count)
    item_scale_new = item_mass / (column_total.reshape(128) / user_count)
    return user_scale, item_scale_new


def solution(mesh):
    in_specs = (
        P("wide", None),
        P(("wide", "narrow"), None),
        P(("wide", "narrow")),
        P("wide"),
        P(("wide", "narrow")),
    )
    out_specs = (P("wide"), P(("wide", "narrow")))
    return jax.shard_map(
        on_device, mesh=mesh, in_specs=in_specs, out_specs=out_specs, check_vma=False
    )
```

```python
import functools
import math

import jax
import jax.numpy as jnp
from jax import lax
from jax.experimental import pallas as pl
from jax.experimental.pallas import tpu as pltpu
from jax.sharding import PartitionSpec as P

MESH = pl.DeviceIdType.MESH
F32 = jnp.float32
BF16 = jnp.bfloat16

NX, NY, NZ = 4, 8, 8
LINE = 2 * NZ
BLOCK = 128
HALF = 64
USERS = 1024
TILE = 512
TILES = 2 * USERS // TILE
PARTS = TILE // 128
WIDTH = 128
SCALE = 2.0 * math.log2(math.e)


def unit_rows(values, axis):
    squares = jnp.sum(values * values, axis=axis, keepdims=True) + 1e-06
    return (values * lax.rsqrt(squares)).astype(BF16)


def body(
    item_count,
    users_hbm, items_hbm, weight_hbm, mass_hbm,
    row_total_ref, column_total_ref,
    users_in, items_in, weight_in, rows, spread, users, kernel, row_acc, row_parts, masses,
    user_rows, column_send, column_y, column_x, column_half,
    in_sem, x_send, x_recv, y_send, y_recv, f_recv, u_send, u_recv, r_send, r_recv,
    cy_send, cy_recv, cx_send, cx_recv,
):
    wide = lax.axis_index("wide")
    narrow = lax.axis_index("narrow")
    y = wide & (NY - 1)
    x = (wide >> 3) & (NX - 1)
    z_lo = wide >> 5
    line = ((narrow >> 1) << 2) | (z_lo << 1) | (narrow & 1)
    wide_no_y = wide - y
    wide_no_x = wide - (x << 3)
    wide_no_z = wide & (NX * NY - 1)

    def at_x(step):
        return (wide_no_x + (((x + step) & (NX - 1)) << 3), narrow)

    def at_y(step):
        return (wide_no_y + ((y + step) & (NY - 1)), narrow)

    def at_line(step):
        other = (line + step) & (LINE - 1)
        return (wide_no_z + (((other >> 1) & 1) << 5), ((other >> 2) << 1) | (other & 1))

    barrier = pltpu.get_barrier_semaphore()

    def greet(partner):
        pl.semaphore_signal(barrier, inc=1, device_id=partner, device_id_type=MESH)

    def greet_line(step, carry):
        greet(at_line(step))
        return carry

    for step in (1, 3, 2):
        greet(at_x(step))
    for step in (1, 7, 2, 6, 3, 5, 4):
        greet(at_y(step))
    lax.fori_loop(1, LINE, greet_line, 0)

    get_items = pltpu.make_async_copy(items_hbm, items_in, in_sem.at[0])
    get_weight = pltpu.make_async_copy(weight_hbm, weight_in, in_sem.at[1])
    get_users = pltpu.make_async_copy(users_hbm, users_in, in_sem.at[2])
    get_mass = pltpu.make_async_copy(mass_hbm, masses.at[z_lo], in_sem.at[3])
    get_items.start()
    get_weight.start()
    get_users.start()
    get_mass.start()

    get_items.wait()
    get_weight.wait()
    rows[0, 0, 0:BLOCK, :] = unit_rows(items_in[...].astype(F32), 1)
    rows[0, 0, BLOCK:BLOCK + 16, :] = jnp.broadcast_to(
        weight_in[...].astype(F32), (16, BLOCK)
    ).astype(BF16)

    pl.semaphore_wait(barrier, NX - 1 + NY - 1 + LINE - 1)

    def remote(src, dst, send, recv, partner):
        return pltpu.make_async_remote_copy(
            src_ref=src, dst_ref=dst, send_sem=send, recv_sem=recv,
            device_id=partner, device_id_type=MESH,
        )

    def settle(part, sem):
        pltpu.make_async_copy(part, part, sem).wait()

    own = rows.at[0, 0]
    left, right, far = at_x(3), at_x(1), at_x(2)

    def y_send_to(hop):
        if hop == 4:
            remote(own, rows.at[0, 7], y_send.at[0], y_recv.at[4], at_y(4)).start()
            return
        remote(own, rows.at[0, 2 * hop - 1], y_send.at[0], y_recv.at[hop], at_y(hop)).start()
        remote(own, rows.at[0, 2 * hop], y_send.at[0], y_recv.at[hop], at_y(NY - hop)).start()

    def slots_of(hop):
        return slice(2 * hop - 1, 2 * hop + 1) if 0 < hop < 4 else slice(7, 8) if hop else slice(0, 1)

    def x_send_of(hop):
        part = rows.at[0, slots_of(hop)]
        remote(part, rows.at[1, slots_of(hop)], x_send.at[0], x_recv.at[hop], right).start()
        remote(part, rows.at[2, slots_of(hop)], x_send.at[0], x_recv.at[hop], left).start()
        if hop in (0, 4):
            remote(part, rows.at[3, slots_of(hop)], x_send.at[0], x_recv.at[hop], far).start()

    def from_y(hop):
        settle(rows.at[0, slots_of(hop)], y_recv.at[hop])
        x_send_of(hop)

    def from_x(hop):
        if hop in (0, 4):
            settle(rows.at[1:4, slots_of(hop)], x_recv.at[hop])
            return
        settle(rows.at[1:3, slots_of(hop)], x_recv.at[hop])
        behind, ahead = 2 * hop - 1, 2 * hop
        remote(rows.at[1, behind], rows.at[3, behind], x_send.at[0], f_recv.at[hop], right).start()
        remote(rows.at[2, ahead], rows.at[3, ahead], x_send.at[0], f_recv.at[hop], left).start()

    def from_far(hop):
        settle(rows.at[3, slots_of(hop)], f_recv.at[hop])

    y_send_to(1)
    x_send_of(0)
    y_send_to(2)
    y_send_to(3)
    y_send_to(4)

    up, down = at_line(2), at_line(LINE - 2)
    get_users.wait()
    get_mass.wait()
    for half, partner in ((0, up), (1, down)):
        values = users_in[half * TILE:(half + 1) * TILE, :].astype(F32).T
        tile = z_lo * 2 + half
        users[tile] = unit_rows(values, 0)
        part = users.at[tile]
        remote(part, part, u_send.at[half], u_recv.at[half], partner).start()
    remote(masses.at[z_lo], masses.at[z_lo], u_send.at[2], u_recv.at[2], up).start()

    from_y(1)
    from_y(2)
    row_acc[...] = jnp.zeros_like(row_acc)

    def unit_of(unit):
        late = jnp.logical_or(unit == 3, unit >= 5)
        column = jnp.where(unit < 3, unit, jnp.where(unit == 3, 0, jnp.where(unit == 4, 3, unit - 4)))
        return column, jnp.where(late, 4, 0)

    def spread_weights(column, first):
        for block in range(4):
            weight = rows[column, first + block, BLOCK:BLOCK + 16, :].astype(F32)[0:1]
            spread[block * BLOCK:(block + 1) * BLOCK] = jnp.broadcast_to(weight, (BLOCK, BLOCK)).T

    def before(at):
        if at == 2:
            from_y(3)
            from_x(0)
            from_x(1)
            from_x(2)
        elif at == 5:
            from_y(4)
        elif at == 6:
            from_x(3)
        elif at == 8:
            from_far(1)
            from_far(2)
        elif at == 10:
            from_x(4)
        elif at == 14:
            from_far(3)

    def compute_step(at, carry):
        unit, later = at >> 1, at & 1
        column, first = unit_of(unit)
        for known in (2, 5, 6, 8, 10, 14):
            @pl.when(at == known)
            def _():
                before(known)

        @pl.when(later == 0)
        def _():
            spread_weights(column, first)

        @pl.when(at == 1)
        def _():
            for half in (0, 1):
                settle(users.at[half], u_recv.at[half])
            settle(masses.at[0], u_recv.at[2])

        block_of_users = (z_lo + later) & 1
        accs = [jnp.zeros((8, TILE), F32) for _ in range(2)]
        for pair in range(2):
            left = jnp.concatenate(
                [rows[column, first + 2 * pair + block, 0:BLOCK, :] for block in range(2)], axis=0
            )
            here = slice(pair * 2 * BLOCK, (pair + 1) * 2 * BLOCK)
            weight = jnp.concatenate([spread[here]] * PARTS, axis=1)
            for part in range(2):
                tile = block_of_users * 2 + part
                scores = jnp.dot(left, users[tile], preferred_element_type=F32)
                values = jnp.exp2(scores * SCALE)
                kernel[unit, tile, here] = values
                weighted = values * weight
                accs[part] += jnp.sum(weighted.reshape(2 * BLOCK // 8, 8, TILE), axis=0)
        for part in range(2):
            row_acc[block_of_users * 2 + part] += accs[part]
        return carry

    lax.fori_loop(0, 16, compute_step, 0)

    for tile in range(TILES):
        total = jnp.sum(row_acc[tile], axis=0, keepdims=True)
        for part in range(PARTS):
            at = tile * PARTS + part
            row_parts[line, at:at + 1, :] = total[:, part * 128:(part + 1) * 128]

    def send_rows(step, carry):
        remote(row_parts.at[line], row_parts.at[line], r_send.at[0], r_recv.at[0],
               at_line(step)).start()
        return carry

    lax.fori_loop(1, LINE, send_rows, 0)
    settle(row_parts.at[0:LINE - 1], r_recv.at[0])
    total = row_parts[0]
    for part in range(1, LINE):
        total = total + row_parts[part]
    scale = masses[...].reshape(16, 128) / (total / item_count)
    for at in range(TILES * PARTS):
        user_rows[at] = jnp.broadcast_to(scale[at:at + 1, :], (8, 128))
    column_half[...] = total.reshape(2, 8, 128)
    row_total_ref[...] = column_half[z_lo]

    def sum_columns(unit, column, first):
        for block in range(4):
            pieces = []
            for half in (0, 1):
                acc = jnp.zeros((HALF // 8, 8, 128), F32)
                for tile in range(TILES):
                    for part in range(PARTS):
                        piece = kernel[unit, tile,
                                       block * BLOCK + half * HALF:block * BLOCK + (half + 1) * HALF,
                                       part * 128:(part + 1) * 128]
                        piece = piece.reshape(HALF // 8, 8, 128)
                        acc = acc + piece * user_rows[tile * PARTS + part]
                pieces.append(acc.reshape(HALF, 128))
            flat = jnp.concatenate(pieces, axis=0).T
            column_send[first + block, column] = jnp.sum(flat, axis=0, keepdims=True)

    def send_columns(slot):
        hop = (slot + 1) // 2
        remote(column_send.at[slot], column_y.at[slot], cy_send.at[0], cy_recv.at[0],
               at_y(NY - hop if slot % 2 else hop)).start()

    def column_step(step, carry):
        column = step & 3
        late = step < 4
        unit = jnp.where(
            late, jnp.where(column == 0, 3, column + 4), jnp.where(column == 3, 4, column)
        )
        sum_columns(unit, column, jnp.where(late, 4, 0))

        @pl.when(step == 3)
        def _():
            for slot in (7, 5, 6, 4):
                send_columns(slot)

        return carry

    lax.fori_loop(0, 8, column_step, 0)
    for slot in (3, 1, 2):
        send_columns(slot)
    column_y[0] = column_send[0]
    settle(column_y.at[1:NY], cy_recv.at[0])
    total = column_y[0]
    for part in range(1, NY):
        total = total + column_y[part]
    column_x[NX] = total
    for column, source, partner in ((3, 3, far), (1, 2, left), (2, 1, right)):
        remote(column_x.at[NX, column], column_x.at[source, 0],
               cx_send.at[0], cx_recv.at[0], partner).start()
    column_x[0, 0] = column_x[NX, 0]
    settle(column_x.at[1:NX, 0], cx_recv.at[0])
    total = column_x[0, 0]
    for part in range(1, NX):
        total = total + column_x[part, 0]
    column_total_ref[...] = total

    settle(rows.at[0, 1:NY], y_send.at[0])
    settle(rows.at[1:NX], x_send.at[0])
    for half in (0, 1):
        settle(users.at[half], u_send.at[half])
    settle(masses.at[0], u_send.at[2])
    settle(row_parts.at[0:LINE - 1], r_send.at[0])
    settle(column_y.at[1:NY], cy_send.at[0])
    settle(column_x.at[1:NX, 0], cx_send.at[0])


def on_device(users, items, item_scale, user_mass, item_mass):
    user_count = users.shape[0] * lax.axis_size("wide")
    item_count = items.shape[0] * lax.axis_size("wide") * lax.axis_size("narrow")
    dma = pltpu.SemaphoreType.DMA
    vmem = pl.BlockSpec(memory_space=pltpu.VMEM)
    row_total, column_total = pl.pallas_call(
        functools.partial(body, item_count),
        out_shape=(
            jax.ShapeDtypeStruct((8, 128), F32),
            jax.ShapeDtypeStruct((1, 128), F32),
        ),
        in_specs=[pl.BlockSpec(memory_space=pl.ANY)] * 4,
        out_specs=(vmem, vmem),
        scratch_shapes=[
            pltpu.VMEM((USERS, WIDTH), BF16),
            pltpu.VMEM((BLOCK, WIDTH), BF16),
            pltpu.VMEM((1, BLOCK), BF16),
            pltpu.VMEM((NX, NY, BLOCK + 16, WIDTH), BF16),
            pltpu.VMEM((4 * BLOCK, BLOCK), F32),
            pltpu.VMEM((TILES, WIDTH, TILE), BF16),
            pltpu.VMEM((NY, TILES, 4 * BLOCK, TILE), F32),
            pltpu.VMEM((TILES, 8, TILE), F32),
            pltpu.VMEM((LINE, 16, 128), F32),
            pltpu.VMEM((2, 8, 128), F32),
            pltpu.VMEM((TILES * PARTS, 8, 128), F32),
            pltpu.VMEM((NY, NX, 1, BLOCK), F32),
            pltpu.VMEM((NY, NX, 1, BLOCK), F32),
            pltpu.VMEM((NX + 1, NX, 1, BLOCK), F32),
            pltpu.VMEM((2, 8, 128), F32),
            dma((4,)),
            dma((1,)), dma((5,)),
            dma((1,)), dma((5,)),
            dma((4,)),
            dma((3,)), dma((3,)),
            dma((1,)), dma((1,)),
            dma((1,)), dma((1,)),
            dma((1,)), dma((1,)),
        ],
        compiler_params=pltpu.CompilerParams(
            collective_id=0, has_side_effects=True, vmem_limit_bytes=56 * 1024 * 1024
        ),
        cost_estimate=pl.CostEstimate(
            flops=2 * 4096 * 2048 * 256, bytes_accessed=1 << 20, transcendentals=4096 * 2048
        ),
        name="scaling",
    )(users, items, item_scale.reshape(1, 128), user_mass.reshape(8, 128))
    user_scale = user_mass / (row_total.reshape(1024) / item_count)
    item_scale_new = item_mass / (column_total.reshape(128) / user_count)
    return user_scale, item_scale_new


def solution(mesh):
    in_specs = (
        P("wide", None),
        P(("wide", "narrow"), None),
        P(("wide", "narrow")),
        P("wide"),
        P(("wide", "narrow")),
    )
    out_specs = (P("wide"), P(("wide", "narrow")))
    return jax.shard_map(
        on_device, mesh=mesh, in_specs=in_specs, out_specs=out_specs, check_vma=False
    )
```

```python
import functools
import math

import jax
import jax.numpy as jnp
from jax import lax
from jax.experimental import pallas as pl
from jax.experimental.pallas import tpu as pltpu
from jax.sharding import PartitionSpec as P

MESH = pl.DeviceIdType.MESH
F32 = jnp.float32
BF16 = jnp.bfloat16

NX, NY, NZ = 4, 8, 8
LINE = 2 * NZ
BLOCK = 128
HALF = 64
USERS = 1024
TILE = 512
TILES = 2 * USERS // TILE
PARTS = TILE // 128
WIDTH = 128
SCALE = 2.0 * math.log2(math.e)


def unit_rows(values, axis):
    squares = jnp.sum(values * values, axis=axis, keepdims=True) + 1e-06
    return (values * lax.rsqrt(squares)).astype(BF16)


def body(
    item_count,
    users_hbm, items_hbm, weight_hbm, mass_hbm,
    row_total_ref, column_total_ref,
    users_in, items_in, weight_in, rows, users, kernel, row_acc, row_parts, masses,
    user_rows, column_send, column_y, column_x, column_half,
    in_sem, x_send, x_recv, y_send, y_recv, f_recv, u_send, u_recv, r_send, r_recv,
    cy_send, cy_recv, cx_send, cx_recv,
):
    wide = lax.axis_index("wide")
    narrow = lax.axis_index("narrow")
    y = wide & (NY - 1)
    x = (wide >> 3) & (NX - 1)
    z_lo = wide >> 5
    line = ((narrow >> 1) << 2) | (z_lo << 1) | (narrow & 1)
    wide_no_y = wide - y
    wide_no_x = wide - (x << 3)
    wide_no_z = wide & (NX * NY - 1)

    def at_x(step):
        return (wide_no_x + (((x + step) & (NX - 1)) << 3), narrow)

    def at_y(step):
        return (wide_no_y + ((y + step) & (NY - 1)), narrow)

    def at_line(step):
        other = (line + step) & (LINE - 1)
        return (wide_no_z + (((other >> 1) & 1) << 5), ((other >> 2) << 1) | (other & 1))

    get_items = pltpu.make_async_copy(items_hbm, items_in, in_sem.at[0])
    get_weight = pltpu.make_async_copy(weight_hbm, weight_in, in_sem.at[1])
    get_users = pltpu.make_async_copy(users_hbm, users_in, in_sem.at[2])
    get_mass = pltpu.make_async_copy(mass_hbm, masses.at[z_lo], in_sem.at[3])
    get_items.start()
    get_weight.start()
    get_users.start()
    get_mass.start()

    barrier = pltpu.get_barrier_semaphore()

    def greet(partner):
        pl.semaphore_signal(barrier, inc=1, device_id=partner, device_id_type=MESH)

    def greet_line(step, carry):
        greet(at_line(step))
        return carry

    for step in (1, 3, 2):
        greet(at_x(step))
    for step in (1, 7, 2, 6, 3, 5, 4):
        greet(at_y(step))
    lax.fori_loop(1, LINE, greet_line, 0)

    get_items.wait()
    get_weight.wait()
    rows[0, 0, 0:BLOCK, :] = unit_rows(items_in[...].astype(F32), 1)
    rows[0, 0, BLOCK:BLOCK + 16, :] = jnp.broadcast_to(
        weight_in[...].astype(F32), (16, BLOCK)
    ).astype(BF16)

    pl.semaphore_wait(barrier, NX - 1 + NY - 1 + LINE - 1)

    def remote(src, dst, send, recv, partner):
        return pltpu.make_async_remote_copy(
            src_ref=src, dst_ref=dst, send_sem=send, recv_sem=recv,
            device_id=partner, device_id_type=MESH,
        )

    def settle(part, sem):
        pltpu.make_async_copy(part, part, sem).wait()

    own = rows.at[0, 0]
    left, right, far = at_x(3), at_x(1), at_x(2)

    def y_send_to(hop):
        if hop == 4:
            remote(own, rows.at[0, 7], y_send.at[0], y_recv.at[4], at_y(4)).start()
            return
        remote(own, rows.at[0, 2 * hop - 1], y_send.at[0], y_recv.at[hop], at_y(hop)).start()
        remote(own, rows.at[0, 2 * hop], y_send.at[0], y_recv.at[hop], at_y(NY - hop)).start()

    def slots_of(hop):
        return slice(2 * hop - 1, 2 * hop + 1) if 0 < hop < 4 else slice(7, 8) if hop else slice(0, 1)

    def x_send_of(hop):
        part = rows.at[0, slots_of(hop)]
        remote(part, rows.at[1, slots_of(hop)], x_send.at[0], x_recv.at[hop], right).start()
        remote(part, rows.at[2, slots_of(hop)], x_send.at[0], x_recv.at[hop], left).start()
        if hop in (0, 4):
            remote(part, rows.at[3, slots_of(hop)], x_send.at[0], x_recv.at[hop], far).start()

    def from_y(hop):
        settle(rows.at[0, slots_of(hop)], y_recv.at[hop])
        x_send_of(hop)

    def from_x(hop):
        if hop in (0, 4):
            settle(rows.at[1:4, slots_of(hop)], x_recv.at[hop])
            return
        settle(rows.at[1:3, slots_of(hop)], x_recv.at[hop])
        behind, ahead = 2 * hop - 1, 2 * hop
        remote(rows.at[1, behind], rows.at[3, behind], x_send.at[0], f_recv.at[hop], right).start()
        remote(rows.at[2, ahead], rows.at[3, ahead], x_send.at[0], f_recv.at[hop], left).start()

    def from_far(hop):
        settle(rows.at[3, slots_of(hop)], f_recv.at[hop])

    y_send_to(1)
    x_send_of(0)
    y_send_to(2)
    y_send_to(3)
    y_send_to(4)

    up, down = at_line(2), at_line(LINE - 2)
    get_users.wait()
    get_mass.wait()
    for half, partner in ((0, up), (1, down)):
        values = users_in[half * TILE:(half + 1) * TILE, :].astype(F32).T
        tile = z_lo * 2 + half
        users[tile] = unit_rows(values, 0)
        part = users.at[tile]
        remote(part, part, u_send.at[half], u_recv.at[half], partner).start()
    remote(masses.at[z_lo], masses.at[z_lo], u_send.at[2], u_recv.at[2], up).start()

    from_y(1)
    from_y(2)
    row_acc[...] = jnp.zeros_like(row_acc)

    def unit_of(unit):
        late = jnp.logical_or(unit == 3, unit >= 5)
        column = jnp.where(unit < 3, unit, jnp.where(unit == 3, 0, jnp.where(unit == 4, 3, unit - 4)))
        return column, jnp.where(late, 4, 0)

    def spread_weight(column, slot):
        weight = rows[column, slot, BLOCK:BLOCK + 16, :].astype(F32)[0:1]
        return jnp.broadcast_to(weight, (BLOCK, BLOCK)).T

    def before(at):
        if at == 2:
            from_y(3)
            from_x(0)
            from_x(1)
            from_x(2)
        elif at == 5:
            from_y(4)
        elif at == 6:
            from_x(3)
        elif at == 8:
            from_far(1)
            from_far(2)
        elif at == 10:
            from_x(4)
        elif at == 14:
            from_far(3)

    def compute_step(at, carry):
        unit, later = at >> 1, at & 1
        column, first = unit_of(unit)
        for known in (2, 5, 6, 8, 10, 14):
            @pl.when(at == known)
            def _():
                before(known)

        @pl.when(at == 1)
        def _():
            for half in (0, 1):
                settle(users.at[half], u_recv.at[half])
            settle(masses.at[0], u_recv.at[2])

        block_of_users = (z_lo + later) & 1
        accs = [jnp.zeros((8, TILE), F32) for _ in range(2)]
        for pair in range(2):
            both = [first + 2 * pair, first + 2 * pair + 1]
            left_rows = jnp.concatenate([rows[column, slot, 0:BLOCK, :] for slot in both], axis=0)
            here = slice(pair * 2 * BLOCK, (pair + 1) * 2 * BLOCK)
            weight = jnp.concatenate([spread_weight(column, slot) for slot in both], axis=0)
            weight = jnp.concatenate([weight] * PARTS, axis=1)
            for part in range(2):
                tile = block_of_users * 2 + part
                scores = jnp.dot(left_rows, users[tile], preferred_element_type=F32)
                values = jnp.exp2(scores * SCALE)
                kernel[unit, tile, here] = values
                weighted = values * weight
                accs[part] += jnp.sum(weighted.reshape(2 * BLOCK // 8, 8, TILE), axis=0)
        for part in range(2):
            row_acc[block_of_users * 2 + part] += accs[part]
        return carry

    lax.fori_loop(0, 16, compute_step, 0)

    for tile in range(TILES):
        total = jnp.sum(row_acc[tile], axis=0, keepdims=True)
        for part in range(PARTS):
            at = tile * PARTS + part
            row_parts[line, at:at + 1, :] = total[:, part * 128:(part + 1) * 128]

    def send_rows(step, carry):
        remote(row_parts.at[line], row_parts.at[line], r_send.at[0], r_recv.at[0],
               at_line(step)).start()
        return carry

    lax.fori_loop(1, LINE, send_rows, 0)
    settle(row_parts.at[0:LINE - 1], r_recv.at[0])
    total = row_parts[0]
    for part in range(1, LINE):
        total = total + row_parts[part]
    scale = masses[...].reshape(16, 128) / (total / item_count)
    for at in range(TILES * PARTS):
        user_rows[at] = jnp.broadcast_to(scale[at:at + 1, :], (8, 128))
    column_half[...] = total.reshape(2, 8, 128)
    row_total_ref[...] = column_half[z_lo]

    def sum_columns(unit, column, first):
        for block in range(4):
            pieces = []
            for half in (0, 1):
                acc = jnp.zeros((HALF // 8, 8, 128), F32)
                for tile in range(TILES):
                    for part in range(PARTS):
                        piece = kernel[unit, tile,
                                       block * BLOCK + half * HALF:block * BLOCK + (half + 1) * HALF,
                                       part * 128:(part + 1) * 128]
                        piece = piece.reshape(HALF // 8, 8, 128)
                        acc = acc + piece * user_rows[tile * PARTS + part]
                pieces.append(acc.reshape(HALF, 128))
            flat = jnp.concatenate(pieces, axis=0).T
            column_send[column, first + block] = jnp.sum(flat, axis=0, keepdims=True)

    def column_step(step, carry):
        turn, late = step >> 1, (step & 1) == 1
        column = jnp.where(turn == 0, 3, jnp.where(turn == 3, 0, turn))
        unit = jnp.where(
            late, jnp.where(column == 0, 3, column + 4), jnp.where(column == 3, 4, column)
        )
        sum_columns(unit, column, jnp.where(late, 4, 0))
        for known, done, source, partner in ((1, 3, 3, far), (3, 1, 2, left), (5, 2, 1, right)):
            @pl.when(step == known)
            def _():
                remote(column_send.at[done], column_x.at[source],
                       cx_send.at[0], cx_recv.at[0], partner).start()

        return carry

    lax.fori_loop(0, 8, column_step, 0)
    settle(column_x.at[1:NX], cx_recv.at[0])
    column_x[0] = column_send[0] + column_x[1] + column_x[2] + column_x[3]
    for slot in (7, 5, 6, 3, 4, 1, 2):
        hop = (slot + 1) // 2
        remote(column_x.at[0, slot], column_y.at[slot], cy_send.at[0], cy_recv.at[0],
               at_y(NY - hop if slot % 2 else hop)).start()
    settle(column_y.at[1:NY], cy_recv.at[0])
    total = column_x[0, 0]
    for part in range(1, NY):
        total = total + column_y[part]
    column_total_ref[...] = total

    settle(rows.at[0, 1:NY], y_send.at[0])
    settle(rows.at[1:NX], x_send.at[0])
    for half in (0, 1):
        settle(users.at[half], u_send.at[half])
    settle(masses.at[0], u_send.at[2])
    settle(row_parts.at[0:LINE - 1], r_send.at[0])
    settle(column_y.at[1:NY], cy_send.at[0])
    settle(column_x.at[1:NX], cx_send.at[0])


def on_device(users, items, item_scale, user_mass, item_mass):
    user_count = users.shape[0] * lax.axis_size("wide")
    item_count = items.shape[0] * lax.axis_size("wide") * lax.axis_size("narrow")
    dma = pltpu.SemaphoreType.DMA
    vmem = pl.BlockSpec(memory_space=pltpu.VMEM)
    row_total, column_total = pl.pallas_call(
        functools.partial(body, item_count),
        out_shape=(
            jax.ShapeDtypeStruct((8, 128), F32),
            jax.ShapeDtypeStruct((1, 128), F32),
        ),
        in_specs=[pl.BlockSpec(memory_space=pl.ANY)] * 4,
        out_specs=(vmem, vmem),
        scratch_shapes=[
            pltpu.VMEM((USERS, WIDTH), BF16),
            pltpu.VMEM((BLOCK, WIDTH), BF16),
            pltpu.VMEM((1, BLOCK), BF16),
            pltpu.VMEM((NX, NY, BLOCK + 16, WIDTH), BF16),
            pltpu.VMEM((TILES, WIDTH, TILE), BF16),
            pltpu.VMEM((NY, TILES, 4 * BLOCK, TILE), F32),
            pltpu.VMEM((TILES, 8, TILE), F32),
            pltpu.VMEM((LINE, 16, 128), F32),
            pltpu.VMEM((2, 8, 128), F32),
            pltpu.VMEM((TILES * PARTS, 8, 128), F32),
            pltpu.VMEM((NX, NY, 1, BLOCK), F32),
            pltpu.VMEM((NY, 1, BLOCK), F32),
            pltpu.VMEM((NX, NY, 1, BLOCK), F32),
            pltpu.VMEM((2, 8, 128), F32),
            dma((4,)),
            dma((1,)), dma((5,)),
            dma((1,)), dma((5,)),
            dma((4,)),
            dma((3,)), dma((3,)),
            dma((1,)), dma((1,)),
            dma((1,)), dma((1,)),
            dma((1,)), dma((1,)),
        ],
        compiler_params=pltpu.CompilerParams(
            collective_id=0, has_side_effects=True, vmem_limit_bytes=56 * 1024 * 1024
        ),
        cost_estimate=pl.CostEstimate(
            flops=2 * 4096 * 2048 * 256, bytes_accessed=1 << 20, transcendentals=4096 * 2048
        ),
        name="scaling",
    )(users, items, item_scale.reshape(1, 128), user_mass.reshape(8, 128))
    user_scale = user_mass / (row_total.reshape(1024) / item_count)
    item_scale_new = item_mass / (column_total.reshape(128) / user_count)
    return user_scale, item_scale_new


def solution(mesh):
    in_specs = (
        P("wide", None),
        P(("wide", "narrow"), None),
        P(("wide", "narrow")),
        P("wide"),
        P(("wide", "narrow")),
    )
    out_specs = (P("wide"), P(("wide", "narrow")))
    return jax.shard_map(
        on_device, mesh=mesh, in_specs=in_specs, out_specs=out_specs, check_vma=False
    )
```

```python
import functools
import math

import jax
import jax.numpy as jnp
from jax import lax
from jax.experimental import pallas as pl
from jax.experimental.pallas import tpu as pltpu
from jax.sharding import PartitionSpec as P

MESH = pl.DeviceIdType.MESH
F32 = jnp.float32
BF16 = jnp.bfloat16

NX, NY, NZ = 4, 8, 8
LINE = 2 * NZ
BLOCK = 128
HALF = 64
USERS = 1024
TILE = 512
TILES = 2 * USERS // TILE
PARTS = TILE // 128
WIDTH = 128
SCALE = 2.0 * math.log2(math.e)


def unit_rows(values, axis):
    squares = jnp.sum(values * values, axis=axis, keepdims=True) + 1e-06
    return (values * lax.rsqrt(squares)).astype(BF16)


def body(
    item_count,
    users_hbm, items_hbm, weight_hbm, mass_hbm,
    row_total_ref, column_total_ref,
    users_in, items_in, weight_in, rows, users, kernel, row_acc, row_parts, masses,
    user_rows, column_send, column_y, column_x, column_half,
    in_sem, x_send, x_recv, y_send, y_recv, f_recv, u_send, u_recv, r_send, r_recv,
    cy_send, cy_recv, cx_send, cx_recv,
):
    wide = lax.axis_index("wide")
    narrow = lax.axis_index("narrow")
    y = wide & (NY - 1)
    x = (wide >> 3) & (NX - 1)
    z_lo = wide >> 5
    line = ((narrow >> 1) << 2) | (z_lo << 1) | (narrow & 1)
    wide_no_y = wide - y
    wide_no_x = wide - (x << 3)
    wide_no_z = wide & (NX * NY - 1)

    def at_x(step):
        return (wide_no_x + (((x + step) & (NX - 1)) << 3), narrow)

    def at_y(step):
        return (wide_no_y + ((y + step) & (NY - 1)), narrow)

    def at_line(step):
        other = (line + step) & (LINE - 1)
        return (wide_no_z + (((other >> 1) & 1) << 5), ((other >> 2) << 1) | (other & 1))

    get_items = pltpu.make_async_copy(items_hbm, items_in, in_sem.at[0])
    get_weight = pltpu.make_async_copy(weight_hbm, weight_in, in_sem.at[1])
    get_users = pltpu.make_async_copy(users_hbm, users_in, in_sem.at[2])
    get_mass = pltpu.make_async_copy(mass_hbm, masses.at[z_lo], in_sem.at[3])
    get_items.start()
    get_weight.start()
    get_users.start()
    get_mass.start()

    barrier = pltpu.get_barrier_semaphore()

    def greet(partner):
        pl.semaphore_signal(barrier, inc=1, device_id=partner, device_id_type=MESH)

    def greet_line(step, carry):
        greet(at_line(step))
        return carry

    for step in (1, 3, 2):
        greet(at_x(step))
    for step in (1, 7, 2, 6, 3, 5, 4):
        greet(at_y(step))
    lax.fori_loop(1, LINE, greet_line, 0)

    get_items.wait()
    get_weight.wait()
    rows[0, 0, 0:BLOCK, :] = unit_rows(items_in[...].astype(F32), 1)
    rows[0, 0, BLOCK:BLOCK + 16, :] = jnp.broadcast_to(
        weight_in[...].astype(F32), (16, BLOCK)
    ).astype(BF16)

    pl.semaphore_wait(barrier, NX - 1 + NY - 1 + LINE - 1)

    def remote(src, dst, send, recv, partner):
        return pltpu.make_async_remote_copy(
            src_ref=src, dst_ref=dst, send_sem=send, recv_sem=recv,
            device_id=partner, device_id_type=MESH,
        )

    def settle(part, sem):
        pltpu.make_async_copy(part, part, sem).wait()

    own = rows.at[0, 0]
    left, right, far = at_x(3), at_x(1), at_x(2)

    def y_send_to(hop):
        if hop == 4:
            remote(own, rows.at[0, 7], y_send.at[0], y_recv.at[4], at_y(4)).start()
            return
        remote(own, rows.at[0, 2 * hop - 1], y_send.at[0], y_recv.at[hop], at_y(hop)).start()
        remote(own, rows.at[0, 2 * hop], y_send.at[0], y_recv.at[hop], at_y(NY - hop)).start()

    def slots_of(hop):
        return slice(2 * hop - 1, 2 * hop + 1) if 0 < hop < 4 else slice(7, 8) if hop else slice(0, 1)

    def x_send_of(hop):
        part = rows.at[0, slots_of(hop)]
        remote(part, rows.at[1, slots_of(hop)], x_send.at[0], x_recv.at[hop], right).start()
        remote(part, rows.at[2, slots_of(hop)], x_send.at[0], x_recv.at[hop], left).start()
        if hop in (0, 4):
            remote(part, rows.at[3, slots_of(hop)], x_send.at[0], x_recv.at[hop], far).start()

    def from_y(hop):
        settle(rows.at[0, slots_of(hop)], y_recv.at[hop])
        x_send_of(hop)

    def from_x(hop):
        if hop in (0, 4):
            settle(rows.at[1:4, slots_of(hop)], x_recv.at[hop])
            return
        settle(rows.at[1:3, slots_of(hop)], x_recv.at[hop])
        behind, ahead = 2 * hop - 1, 2 * hop
        remote(rows.at[1, behind], rows.at[3, behind], x_send.at[0], f_recv.at[hop], right).start()
        remote(rows.at[2, ahead], rows.at[3, ahead], x_send.at[0], f_recv.at[hop], left).start()

    def from_far(hop):
        settle(rows.at[3, slots_of(hop)], f_recv.at[hop])

    y_send_to(1)
    x_send_of(0)
    y_send_to(2)
    y_send_to(3)
    y_send_to(4)

    up, down = at_line(2), at_line(LINE - 2)
    get_users.wait()
    get_mass.wait()
    for half, partner in ((0, up), (1, down)):
        values = users_in[half * TILE:(half + 1) * TILE, :].astype(F32).T
        tile = z_lo * 2 + half
        users[tile] = unit_rows(values, 0)
        part = users.at[tile]
        remote(part, part, u_send.at[half], u_recv.at[half], partner).start()
    remote(masses.at[z_lo], masses.at[z_lo], u_send.at[2], u_recv.at[2], up).start()

    from_y(1)
    from_y(2)
    row_acc[...] = jnp.zeros_like(row_acc)

    def unit_of(unit):
        late = jnp.logical_or(unit == 3, unit >= 5)
        column = jnp.where(unit < 3, unit, jnp.where(unit == 3, 0, jnp.where(unit == 4, 3, unit - 4)))
        return column, jnp.where(late, 4, 0)

    def spread_weight(column, slot):
        weight = rows[column, slot, BLOCK:BLOCK + 16, :].astype(F32)[0:1]
        return jnp.broadcast_to(weight, (BLOCK, BLOCK)).T

    def before(at):
        if at == 2:
            from_y(3)
            from_x(0)
            from_x(1)
            from_x(2)
        elif at == 5:
            from_y(4)
        elif at == 6:
            from_x(3)
        elif at == 8:
            from_far(1)
            from_far(2)
        elif at == 10:
            from_x(4)
        elif at == 14:
            from_far(3)

    def compute_step(at, carry):
        unit, later = at >> 1, at & 1
        column, first = unit_of(unit)
        for known in (2, 5, 6, 8, 10, 14):
            @pl.when(at == known)
            def _():
                before(known)

        @pl.when(at == 1)
        def _():
            for half in (0, 1):
                settle(users.at[half], u_recv.at[half])
            settle(masses.at[0], u_recv.at[2])

        block_of_users = (z_lo + later) & 1
        wide_of = TILE // 2
        accs = [jnp.zeros((8, wide_of), F32) for _ in range(4)]
        for block in range(4):
            left_rows = rows[column, first + block, 0:BLOCK, :]
            weight = spread_weight(column, first + block)
            weight = jnp.concatenate([weight] * (wide_of // 128), axis=1)
            here = slice(block * BLOCK, (block + 1) * BLOCK)
            for part in range(4):
                tile = block_of_users * 2 + part // 2
                there = slice(part % 2 * wide_of, (part % 2 + 1) * wide_of)
                scores = jnp.dot(left_rows, users[tile, :, there], preferred_element_type=F32)
                values = jnp.exp2(scores * SCALE)
                kernel[unit, tile, here, there] = values
                weighted = (values * weight).reshape(BLOCK // 8, 8, wide_of)
                accs[part] += jnp.sum(weighted, axis=0)
        for part in range(4):
            there = slice(part % 2 * wide_of, (part % 2 + 1) * wide_of)
            row_acc[block_of_users * 2 + part // 2, :, there] += accs[part]
        return carry

    lax.fori_loop(0, 16, compute_step, 0)

    for tile in range(TILES):
        total = jnp.sum(row_acc[tile], axis=0, keepdims=True)
        for part in range(PARTS):
            at = tile * PARTS + part
            row_parts[line, at:at + 1, :] = total[:, part * 128:(part + 1) * 128]

    def send_rows(step, carry):
        remote(row_parts.at[line], row_parts.at[line], r_send.at[0], r_recv.at[0],
               at_line(step)).start()
        return carry

    lax.fori_loop(1, LINE, send_rows, 0)
    settle(row_parts.at[0:LINE - 1], r_recv.at[0])
    total = row_parts[0]
    for part in range(1, LINE):
        total = total + row_parts[part]
    scale = masses[...].reshape(16, 128) / (total / item_count)
    for at in range(TILES * PARTS):
        user_rows[at] = jnp.broadcast_to(scale[at:at + 1, :], (8, 128))
    column_half[...] = total.reshape(2, 8, 128)
    row_total_ref[...] = column_half[z_lo]

    def sum_columns(unit, column, first):
        for block in range(4):
            pieces = []
            for half in (0, 1):
                acc = jnp.zeros((HALF // 8, 8, 128), F32)
                for tile in range(TILES):
                    for part in range(PARTS):
                        piece = kernel[unit, tile,
                                       block * BLOCK + half * HALF:block * BLOCK + (half + 1) * HALF,
                                       part * 128:(part + 1) * 128]
                        piece = piece.reshape(HALF // 8, 8, 128)
                        acc = acc + piece * user_rows[tile * PARTS + part]
                pieces.append(acc.reshape(HALF, 128))
            flat = jnp.concatenate(pieces, axis=0).T
            column_send[column, first + block] = jnp.sum(flat, axis=0, keepdims=True)

    def column_step(step, carry):
        turn, late = step >> 1, (step & 1) == 1
        column = jnp.where(turn == 0, 3, jnp.where(turn == 3, 0, turn))
        unit = jnp.where(
            late, jnp.where(column == 0, 3, column + 4), jnp.where(column == 3, 4, column)
        )
        sum_columns(unit, column, jnp.where(late, 4, 0))
        for known, done, source, partner in ((1, 3, 3, far), (3, 1, 2, left), (5, 2, 1, right)):
            @pl.when(step == known)
            def _():
                remote(column_send.at[done], column_x.at[source],
                       cx_send.at[0], cx_recv.at[0], partner).start()

        return carry

    lax.fori_loop(0, 8, column_step, 0)
    settle(column_x.at[1:NX], cx_recv.at[0])
    column_x[0] = column_send[0] + column_x[1] + column_x[2] + column_x[3]
    for slot in (7, 5, 6, 3, 4, 1, 2):
        hop = (slot + 1) // 2
        remote(column_x.at[0, slot], column_y.at[slot], cy_send.at[0], cy_recv.at[0],
               at_y(NY - hop if slot % 2 else hop)).start()
    settle(column_y.at[1:NY], cy_recv.at[0])
    total = column_x[0, 0]
    for part in range(1, NY):
        total = total + column_y[part]
    column_total_ref[...] = total

    settle(rows.at[0, 1:NY], y_send.at[0])
    settle(rows.at[1:NX], x_send.at[0])
    for half in (0, 1):
        settle(users.at[half], u_send.at[half])
    settle(masses.at[0], u_send.at[2])
    settle(row_parts.at[0:LINE - 1], r_send.at[0])
    settle(column_y.at[1:NY], cy_send.at[0])
    settle(column_x.at[1:NX], cx_send.at[0])


def on_device(users, items, item_scale, user_mass, item_mass):
    user_count = users.shape[0] * lax.axis_size("wide")
    item_count = items.shape[0] * lax.axis_size("wide") * lax.axis_size("narrow")
    dma = pltpu.SemaphoreType.DMA
    vmem = pl.BlockSpec(memory_space=pltpu.VMEM)
    row_total, column_total = pl.pallas_call(
        functools.partial(body, item_count),
        out_shape=(
            pltpu.VMEM((8, 128), F32),
            pltpu.VMEM((1, 128), F32),
        ),
        in_specs=[pl.BlockSpec(memory_space=pl.ANY)] * 4,
        out_specs=(vmem, vmem),
        scratch_shapes=[
            pltpu.VMEM((USERS, WIDTH), BF16),
            pltpu.VMEM((BLOCK, WIDTH), BF16),
            pltpu.VMEM((1, BLOCK), BF16),
            pltpu.VMEM((NX, NY, BLOCK + 16, WIDTH), BF16),
            pltpu.VMEM((TILES, WIDTH, TILE), BF16),
            pltpu.VMEM((NY, TILES, 4 * BLOCK, TILE), F32),
            pltpu.VMEM((TILES, 8, TILE), F32),
            pltpu.VMEM((LINE, 16, 128), F32),
            pltpu.VMEM((2, 8, 128), F32),
            pltpu.VMEM((TILES * PARTS, 8, 128), F32),
            pltpu.VMEM((NX, NY, 1, BLOCK), F32),
            pltpu.VMEM((NY, 1, BLOCK), F32),
            pltpu.VMEM((NX, NY, 1, BLOCK), F32),
            pltpu.VMEM((2, 8, 128), F32),
            dma((4,)),
            dma((1,)), dma((5,)),
            dma((1,)), dma((5,)),
            dma((4,)),
            dma((3,)), dma((3,)),
            dma((1,)), dma((1,)),
            dma((1,)), dma((1,)),
            dma((1,)), dma((1,)),
        ],
        compiler_params=pltpu.CompilerParams(
            collective_id=0, has_side_effects=True, vmem_limit_bytes=56 * 1024 * 1024
        ),
        cost_estimate=pl.CostEstimate(
            flops=2 * 4096 * 2048 * 256, bytes_accessed=1 << 20, transcendentals=4096 * 2048
        ),
        name="scaling",
    )(users, items, item_scale.reshape(1, 128), user_mass.reshape(8, 128))
    user_scale = user_mass / (row_total.reshape(1024) / item_count)
    item_scale_new = item_mass / (column_total.reshape(128) / user_count)
    return user_scale, item_scale_new


def solution(mesh):
    in_specs = (
        P("wide", None),
        P(("wide", "narrow"), None),
        P(("wide", "narrow")),
        P("wide"),
        P(("wide", "narrow")),
    )
    out_specs = (P("wide"), P(("wide", "narrow")))
    return jax.shard_map(
        on_device, mesh=mesh, in_specs=in_specs, out_specs=out_specs, check_vma=False
    )
```

```python
import functools
import math

import jax
import jax.numpy as jnp
from jax import lax
from jax.experimental import pallas as pl
from jax.experimental.pallas import tpu as pltpu
from jax.sharding import PartitionSpec as P

MESH = pl.DeviceIdType.MESH
F32 = jnp.float32
BF16 = jnp.bfloat16

NX, NY, NZ = 4, 8, 8
LINE = 2 * NZ
BLOCK = 128
HALF = 64
USERS = 1024
TILE = 512
TILES = 2 * USERS // TILE
PARTS = TILE // 128
WIDTH = 128
SCALE = 2.0 * math.log2(math.e)


def unit_rows(values, axis):
    squares = jnp.sum(values * values, axis=axis, keepdims=True) + 1e-06
    return (values * lax.rsqrt(squares)).astype(BF16)


def body(
    item_count,
    users_hbm, items_hbm, weight_hbm, mass_hbm,
    row_total_ref, column_total_ref,
    users_in, items_in, weight_in, rows, users, kernel, row_acc, row_parts, masses,
    user_rows, column_send, column_y, column_x, column_half,
    in_sem, x_send, x_recv, y_send, y_recv, f_recv, u_send, u_recv, r_send, r_recv,
    cy_send, cy_recv, cx_send, cx_recv,
):
    wide = lax.axis_index("wide")
    narrow = lax.axis_index("narrow")
    y = wide & (NY - 1)
    x = (wide >> 3) & (NX - 1)
    z_lo = wide >> 5
    line = ((narrow >> 1) << 2) | (z_lo << 1) | (narrow & 1)
    wide_no_y = wide - y
    wide_no_x = wide - (x << 3)
    wide_no_z = wide & (NX * NY - 1)

    def at_x(step):
        return (wide_no_x + (((x + step) & (NX - 1)) << 3), narrow)

    def at_y(step):
        return (wide_no_y + ((y + step) & (NY - 1)), narrow)

    def at_line(step):
        other = (line + step) & (LINE - 1)
        return (wide_no_z + (((other >> 1) & 1) << 5), ((other >> 2) << 1) | (other & 1))

    get_items = pltpu.make_async_copy(items_hbm, items_in, in_sem.at[0])
    get_weight = pltpu.make_async_copy(weight_hbm, weight_in, in_sem.at[1])
    get_users = pltpu.make_async_copy(users_hbm, users_in, in_sem.at[2])
    get_mass = pltpu.make_async_copy(mass_hbm, masses.at[z_lo], in_sem.at[3])
    get_items.start()
    get_weight.start()
    get_users.start()
    get_mass.start()

    barrier = pltpu.get_barrier_semaphore()

    def greet(partner):
        pl.semaphore_signal(barrier, inc=1, device_id=partner, device_id_type=MESH)

    def greet_line(step, carry):
        greet(at_line(step))
        return carry

    for step in (1, 3, 2):
        greet(at_x(step))
    for step in (1, 7, 2, 6, 3, 5, 4):
        greet(at_y(step))
    lax.fori_loop(1, LINE, greet_line, 0)

    get_items.wait()
    get_weight.wait()
    rows[0, 0, 0:BLOCK, :] = unit_rows(items_in[...].astype(F32), 1)
    rows[0, 0, BLOCK:BLOCK + 16, :] = jnp.broadcast_to(
        weight_in[...].astype(F32), (16, BLOCK)
    ).astype(BF16)

    pl.semaphore_wait(barrier, NX - 1 + NY - 1 + LINE - 1)

    def remote(src, dst, send, recv, partner):
        return pltpu.make_async_remote_copy(
            src_ref=src, dst_ref=dst, send_sem=send, recv_sem=recv,
            device_id=partner, device_id_type=MESH,
        )

    def settle(part, sem):
        pltpu.make_async_copy(part, part, sem).wait()

    own = rows.at[0, 0]
    left, right, far = at_x(3), at_x(1), at_x(2)

    def y_send_to(hop):
        if hop == 4:
            remote(own, rows.at[0, 7], y_send.at[0], y_recv.at[4], at_y(4)).start()
            return
        remote(own, rows.at[0, 2 * hop - 1], y_send.at[0], y_recv.at[hop], at_y(hop)).start()
        remote(own, rows.at[0, 2 * hop], y_send.at[0], y_recv.at[hop], at_y(NY - hop)).start()

    def slots_of(hop):
        return slice(2 * hop - 1, 2 * hop + 1) if 0 < hop < 4 else slice(7, 8) if hop else slice(0, 1)

    def x_send_of(hop):
        part = rows.at[0, slots_of(hop)]
        remote(part, rows.at[1, slots_of(hop)], x_send.at[0], x_recv.at[hop], right).start()
        remote(part, rows.at[2, slots_of(hop)], x_send.at[0], x_recv.at[hop], left).start()
        if hop in (0, 4):
            remote(part, rows.at[3, slots_of(hop)], x_send.at[0], x_recv.at[hop], far).start()

    def from_y(hop):
        settle(rows.at[0, slots_of(hop)], y_recv.at[hop])
        x_send_of(hop)

    def from_x(hop):
        if hop in (0, 4):
            settle(rows.at[1:4, slots_of(hop)], x_recv.at[hop])
            return
        settle(rows.at[1:3, slots_of(hop)], x_recv.at[hop])
        behind, ahead = 2 * hop - 1, 2 * hop
        remote(rows.at[1, behind], rows.at[3, behind], x_send.at[0], f_recv.at[hop], right).start()
        remote(rows.at[2, ahead], rows.at[3, ahead], x_send.at[0], f_recv.at[hop], left).start()

    def from_far(hop):
        settle(rows.at[3, slots_of(hop)], f_recv.at[hop])

    y_send_to(1)
    x_send_of(0)
    y_send_to(2)
    y_send_to(3)
    y_send_to(4)

    up, down = at_line(2), at_line(LINE - 2)
    get_users.wait()
    get_mass.wait()
    for half, partner in ((0, up), (1, down)):
        values = users_in[half * TILE:(half + 1) * TILE, :].T.astype(F32)
        tile = z_lo * 2 + half
        users[tile] = unit_rows(values, 0)
        part = users.at[tile]
        remote(part, part, u_send.at[half], u_recv.at[half], partner).start()
    remote(masses.at[z_lo], masses.at[z_lo], u_send.at[2], u_recv.at[2], up).start()

    from_y(1)
    from_y(2)
    row_acc[...] = jnp.zeros_like(row_acc)

    def unit_of(unit):
        late = jnp.logical_or(unit == 3, unit >= 5)
        column = jnp.where(unit < 3, unit, jnp.where(unit == 3, 0, jnp.where(unit == 4, 3, unit - 4)))
        return column, jnp.where(late, 4, 0)

    def spread_weight(column, slot):
        weight = rows[column, slot, BLOCK:BLOCK + 16, :]
        return jnp.concatenate([weight] * (BLOCK // 16), axis=0).T.astype(F32)

    def before(at):
        if at == 2:
            from_y(3)
            from_x(0)
            from_x(1)
            from_x(2)
        elif at == 5:
            from_y(4)
        elif at == 6:
            from_x(3)
        elif at == 8:
            from_far(1)
            from_far(2)
        elif at == 10:
            from_x(4)
        elif at == 14:
            from_far(3)

    def compute_step(at, carry):
        unit, later = at >> 1, at & 1
        column, first = unit_of(unit)
        for known in (2, 5, 6, 8, 10, 14):
            @pl.when(at == known)
            def _():
                before(known)

        @pl.when(at == 1)
        def _():
            for half in (0, 1):
                settle(users.at[half], u_recv.at[half])
            settle(masses.at[0], u_recv.at[2])

        block_of_users = (z_lo + later) & 1
        wide_of = TILE // 2
        accs = [jnp.zeros((8, wide_of), F32) for _ in range(4)]
        for block in range(4):
            left_rows = rows[column, first + block, 0:BLOCK, :]
            weight = spread_weight(column, first + block)
            weight = jnp.concatenate([weight] * (wide_of // 128), axis=1)
            here = slice(block * BLOCK, (block + 1) * BLOCK)
            for part in range(4):
                tile = block_of_users * 2 + part // 2
                there = slice(part % 2 * wide_of, (part % 2 + 1) * wide_of)
                scores = jnp.dot(left_rows, users[tile, :, there], preferred_element_type=F32)
                values = jnp.exp2(scores * SCALE)
                kernel[unit, tile, here, there] = values
                weighted = (values * weight).reshape(BLOCK // 8, 8, wide_of)
                accs[part] += jnp.sum(weighted, axis=0)
        for part in range(4):
            there = slice(part % 2 * wide_of, (part % 2 + 1) * wide_of)
            row_acc[block_of_users * 2 + part // 2, :, there] += accs[part]
        return carry

    lax.fori_loop(0, 16, compute_step, 0)

    for tile in range(TILES):
        total = jnp.sum(row_acc[tile], axis=0, keepdims=True)
        for part in range(PARTS):
            at = tile * PARTS + part
            row_parts[line, at:at + 1, :] = total[:, part * 128:(part + 1) * 128]

    def send_rows(step, carry):
        remote(row_parts.at[line], row_parts.at[line], r_send.at[0], r_recv.at[0],
               at_line(step)).start()
        return carry

    lax.fori_loop(1, LINE, send_rows, 0)
    settle(row_parts.at[0:LINE - 1], r_recv.at[0])
    total = row_parts[0]
    for part in range(1, LINE):
        total = total + row_parts[part]
    scale = masses[...].reshape(16, 128) / (total / item_count)
    for at in range(TILES * PARTS):
        user_rows[at] = jnp.broadcast_to(scale[at:at + 1, :], (8, 128))
    column_half[...] = total.reshape(2, 8, 128)
    row_total_ref[...] = column_half[z_lo]

    def sum_columns(unit, column, first):
        for block in range(4):
            pieces = []
            for half in (0, 1):
                acc = jnp.zeros((HALF // 8, 8, 128), F32)
                for tile in range(TILES):
                    for part in range(PARTS):
                        piece = kernel[unit, tile,
                                       block * BLOCK + half * HALF:block * BLOCK + (half + 1) * HALF,
                                       part * 128:(part + 1) * 128]
                        piece = piece.reshape(HALF // 8, 8, 128)
                        acc = acc + piece * user_rows[tile * PARTS + part]
                pieces.append(acc.reshape(HALF, 128))
            flat = jnp.concatenate(pieces, axis=0).T
            column_send[column, first + block] = jnp.sum(flat, axis=0, keepdims=True)

    def column_step(step, carry):
        turn, late = step >> 1, (step & 1) == 1
        column = jnp.where(turn == 0, 3, jnp.where(turn == 3, 0, turn))
        unit = jnp.where(
            late, jnp.where(column == 0, 3, column + 4), jnp.where(column == 3, 4, column)
        )
        sum_columns(unit, column, jnp.where(late, 4, 0))
        for known, done, source, partner in ((1, 3, 3, far), (3, 1, 2, left), (5, 2, 1, right)):
            @pl.when(step == known)
            def _():
                remote(column_send.at[done], column_x.at[source],
                       cx_send.at[0], cx_recv.at[0], partner).start()

        return carry

    lax.fori_loop(0, 8, column_step, 0)
    settle(column_x.at[1:NX], cx_recv.at[0])
    column_x[0] = column_send[0] + column_x[1] + column_x[2] + column_x[3]
    for slot in (7, 5, 6, 3, 4, 1, 2):
        hop = (slot + 1) // 2
        remote(column_x.at[0, slot], column_y.at[slot], cy_send.at[0], cy_recv.at[0],
               at_y(NY - hop if slot % 2 else hop)).start()
    settle(column_y.at[1:NY], cy_recv.at[0])
    total = column_x[0, 0]
    for part in range(1, NY):
        total = total + column_y[part]
    column_total_ref[...] = total

    settle(rows.at[0, 1:NY], y_send.at[0])
    settle(rows.at[1:NX], x_send.at[0])
    for half in (0, 1):
        settle(users.at[half], u_send.at[half])
    settle(masses.at[0], u_send.at[2])
    settle(row_parts.at[0:LINE - 1], r_send.at[0])
    settle(column_y.at[1:NY], cy_send.at[0])
    settle(column_x.at[1:NX], cx_send.at[0])


def on_device(users, items, item_scale, user_mass, item_mass):
    user_count = users.shape[0] * lax.axis_size("wide")
    item_count = items.shape[0] * lax.axis_size("wide") * lax.axis_size("narrow")
    dma = pltpu.SemaphoreType.DMA
    vmem = pl.BlockSpec(memory_space=pltpu.VMEM)
    row_total, column_total = pl.pallas_call(
        functools.partial(body, item_count),
        out_shape=(
            pltpu.VMEM((8, 128), F32),
            pltpu.VMEM((1, 128), F32),
        ),
        in_specs=[pl.BlockSpec(memory_space=pl.ANY)] * 4,
        out_specs=(vmem, vmem),
        scratch_shapes=[
            pltpu.VMEM((USERS, WIDTH), BF16),
            pltpu.VMEM((BLOCK, WIDTH), BF16),
            pltpu.VMEM((1, BLOCK), BF16),
            pltpu.VMEM((NX, NY, BLOCK + 16, WIDTH), BF16),
            pltpu.VMEM((TILES, WIDTH, TILE), BF16),
            pltpu.VMEM((NY, TILES, 4 * BLOCK, TILE), F32),
            pltpu.VMEM((TILES, 8, TILE), F32),
            pltpu.VMEM((LINE, 16, 128), F32),
            pltpu.VMEM((2, 8, 128), F32),
            pltpu.VMEM((TILES * PARTS, 8, 128), F32),
            pltpu.VMEM((NX, NY, 1, BLOCK), F32),
            pltpu.VMEM((NY, 1, BLOCK), F32),
            pltpu.VMEM((NX, NY, 1, BLOCK), F32),
            pltpu.VMEM((2, 8, 128), F32),
            dma((4,)),
            dma((1,)), dma((5,)),
            dma((1,)), dma((5,)),
            dma((4,)),
            dma((3,)), dma((3,)),
            dma((1,)), dma((1,)),
            dma((1,)), dma((1,)),
            dma((1,)), dma((1,)),
        ],
        compiler_params=pltpu.CompilerParams(
            collective_id=0, has_side_effects=True, vmem_limit_bytes=56 * 1024 * 1024
        ),
        cost_estimate=pl.CostEstimate(
            flops=2 * 4096 * 2048 * 256, bytes_accessed=1 << 20, transcendentals=4096 * 2048
        ),
        name="scaling",
    )(users, items, item_scale.reshape(1, 128), user_mass.reshape(8, 128))
    user_scale = user_mass / (row_total.reshape(1024) / item_count)
    item_scale_new = item_mass / (column_total.reshape(128) / user_count)
    return user_scale, item_scale_new


def solution(mesh):
    in_specs = (
        P("wide", None),
        P(("wide", "narrow"), None),
        P(("wide", "narrow")),
        P("wide"),
        P(("wide", "narrow")),
    )
    out_specs = (P("wide"), P(("wide", "narrow")))
    return jax.shard_map(
        on_device, mesh=mesh, in_specs=in_specs, out_specs=out_specs, check_vma=False
    )
```

```python
import functools
import math

import jax
import jax.numpy as jnp
from jax import lax
from jax.experimental import pallas as pl
from jax.experimental.pallas import tpu as pltpu
from jax.sharding import PartitionSpec as P

MESH = pl.DeviceIdType.MESH
F32 = jnp.float32
BF16 = jnp.bfloat16

NX, NY, NZ = 4, 8, 8
LINE = 2 * NZ
BLOCK = 128
HALF = 64
USERS = 1024
TILE = 512
TILES = 2 * USERS // TILE
PARTS = TILE // 128
WIDTH = 128
SCALE = 2.0 * math.log2(math.e)


def unit_rows(values, axis):
    squares = jnp.sum(values * values, axis=axis, keepdims=True) + 1e-06
    return (values * lax.rsqrt(squares)).astype(BF16)


def body(
    item_count,
    users_hbm, items_hbm, weight_hbm, mass_hbm,
    row_total_ref, column_total_ref,
    users_in, items_in, weight_in, rows, users, kernel, row_acc, row_parts, masses,
    user_rows, column_send, column_y, column_x, column_half,
    in_sem, x_send, x_recv, y_send, y_recv, f_recv, u_send, u_recv, r_send, r_recv,
    cy_send, cy_recv, cx_send, cx_recv,
):
    wide = lax.axis_index("wide")
    narrow = lax.axis_index("narrow")
    y = wide & (NY - 1)
    x = (wide >> 3) & (NX - 1)
    z_lo = wide >> 5
    line = ((narrow >> 1) << 2) | (z_lo << 1) | (narrow & 1)
    wide_no_y = wide - y
    wide_no_x = wide - (x << 3)
    wide_no_z = wide & (NX * NY - 1)

    def at_x(step):
        return (wide_no_x + (((x + step) & (NX - 1)) << 3), narrow)

    def at_y(step):
        return (wide_no_y + ((y + step) & (NY - 1)), narrow)

    def at_line(step):
        other = (line + step) & (LINE - 1)
        return (wide_no_z + (((other >> 1) & 1) << 5), ((other >> 2) << 1) | (other & 1))

    get_items = pltpu.make_async_copy(items_hbm, items_in, in_sem.at[0])
    get_weight = pltpu.make_async_copy(weight_hbm, weight_in, in_sem.at[1])
    get_users = pltpu.make_async_copy(users_hbm, users_in, in_sem.at[2])
    get_mass = pltpu.make_async_copy(mass_hbm, masses.at[z_lo], in_sem.at[3])
    get_items.start()
    get_weight.start()
    get_users.start()
    get_mass.start()

    barrier = pltpu.get_barrier_semaphore()

    def greet(partner):
        pl.semaphore_signal(barrier, inc=1, device_id=partner, device_id_type=MESH)

    def greet_line(step, carry):
        greet(at_line(step))
        return carry

    for step in (1, 3, 2):
        greet(at_x(step))
    for step in (1, 7, 2, 6, 3, 5, 4):
        greet(at_y(step))
    lax.fori_loop(1, LINE, greet_line, 0)

    get_items.wait()
    get_weight.wait()
    rows[0, 0, 0:BLOCK, :] = unit_rows(items_in[...].astype(F32), 1)
    rows[0, 0, BLOCK:BLOCK + 16, :] = jnp.broadcast_to(
        weight_in[...].astype(F32), (16, BLOCK)
    ).astype(BF16)

    pl.semaphore_wait(barrier, NX - 1 + NY - 1 + LINE - 1)

    def remote(src, dst, send, recv, partner):
        return pltpu.make_async_remote_copy(
            src_ref=src, dst_ref=dst, send_sem=send, recv_sem=recv,
            device_id=partner, device_id_type=MESH,
        )

    def settle(part, sem):
        pltpu.make_async_copy(part, part, sem).wait()

    own = rows.at[0, 0]
    left, right, far = at_x(3), at_x(1), at_x(2)

    def y_send_to(hop):
        if hop == 4:
            remote(own, rows.at[0, 7], y_send.at[0], y_recv.at[4], at_y(4)).start()
            return
        remote(own, rows.at[0, 2 * hop - 1], y_send.at[0], y_recv.at[hop], at_y(hop)).start()
        remote(own, rows.at[0, 2 * hop], y_send.at[0], y_recv.at[hop], at_y(NY - hop)).start()

    def slots_of(hop):
        return slice(2 * hop - 1, 2 * hop + 1) if 0 < hop < 4 else slice(7, 8) if hop else slice(0, 1)

    def x_send_of(hop):
        part = rows.at[0, slots_of(hop)]
        remote(part, rows.at[1, slots_of(hop)], x_send.at[0], x_recv.at[hop], right).start()
        remote(part, rows.at[2, slots_of(hop)], x_send.at[0], x_recv.at[hop], left).start()
        if hop in (0, 4):
            remote(part, rows.at[3, slots_of(hop)], x_send.at[0], x_recv.at[hop], far).start()

    def from_y(hop):
        settle(rows.at[0, slots_of(hop)], y_recv.at[hop])
        x_send_of(hop)

    def from_x(hop):
        if hop in (0, 4):
            settle(rows.at[1:4, slots_of(hop)], x_recv.at[hop])
            return
        settle(rows.at[1:3, slots_of(hop)], x_recv.at[hop])
        behind, ahead = 2 * hop - 1, 2 * hop
        remote(rows.at[1, behind], rows.at[3, behind], x_send.at[0], f_recv.at[hop], right).start()
        remote(rows.at[2, ahead], rows.at[3, ahead], x_send.at[0], f_recv.at[hop], left).start()

    def from_far(hop):
        settle(rows.at[3, slots_of(hop)], f_recv.at[hop])

    y_send_to(1)
    x_send_of(0)
    y_send_to(2)

    up, down = at_line(2), at_line(LINE - 2)
    get_users.wait()
    get_mass.wait()
    for half, partner in ((0, up), (1, down)):
        values = users_in[half * TILE:(half + 1) * TILE, :].T.astype(F32)
        tile = z_lo * 2 + half
        users[tile] = unit_rows(values, 0)
        part = users.at[tile]
        remote(part, part, u_send.at[half], u_recv.at[half], partner).start()
    remote(masses.at[z_lo], masses.at[z_lo], u_send.at[2], u_recv.at[2], up).start()

    from_y(1)
    y_send_to(3)
    y_send_to(4)
    from_y(2)
    row_acc[...] = jnp.zeros_like(row_acc)

    def unit_of(unit):
        late = jnp.logical_or(unit == 3, unit >= 5)
        column = jnp.where(unit < 3, unit, jnp.where(unit == 3, 0, jnp.where(unit == 4, 3, unit - 4)))
        return column, jnp.where(late, 4, 0)

    def spread_weight(column, slot):
        weight = rows[column, slot, BLOCK:BLOCK + 16, :]
        return jnp.concatenate([weight] * (BLOCK // 16), axis=0).T.astype(F32)

    def before(at):
        if at == 2:
            from_x(0)
            from_x(1)
            from_x(2)
        elif at == 3:
            from_y(3)
        elif at == 5:
            from_y(4)
        elif at == 6:
            from_x(3)
        elif at == 8:
            from_far(1)
            from_far(2)
        elif at == 10:
            from_x(4)
        elif at == 14:
            from_far(3)

    def compute_step(at, carry):
        unit, later = at >> 1, at & 1
        column, first = unit_of(unit)
        for known in (2, 3, 5, 6, 8, 10, 14):
            @pl.when(at == known)
            def _():
                before(known)

        @pl.when(at == 1)
        def _():
            for half in (0, 1):
                settle(users.at[half], u_recv.at[half])
            settle(masses.at[0], u_recv.at[2])

        block_of_users = (z_lo + later) & 1
        wide_of = TILE // 2
        accs = [jnp.zeros((8, wide_of), F32) for _ in range(4)]
        for block in range(4):
            left_rows = rows[column, first + block, 0:BLOCK, :]
            weight = spread_weight(column, first + block)
            weight = jnp.concatenate([weight] * (wide_of // 128), axis=1)
            here = slice(block * BLOCK, (block + 1) * BLOCK)
            for part in range(4):
                tile = block_of_users * 2 + part // 2
                there = slice(part % 2 * wide_of, (part % 2 + 1) * wide_of)
                scores = jnp.dot(left_rows, users[tile, :, there], preferred_element_type=F32)
                values = jnp.exp2(scores * SCALE)
                kernel[unit, tile, here, there] = values
                weighted = (values * weight).reshape(BLOCK // 8, 8, wide_of)
                accs[part] += jnp.sum(weighted, axis=0)
        for part in range(4):
            there = slice(part % 2 * wide_of, (part % 2 + 1) * wide_of)
            row_acc[block_of_users * 2 + part // 2, :, there] += accs[part]
        return carry

    lax.fori_loop(0, 16, compute_step, 0)

    for tile in range(TILES):
        total = jnp.sum(row_acc[tile], axis=0, keepdims=True)
        for part in range(PARTS):
            at = tile * PARTS + part
            row_parts[line, at:at + 1, :] = total[:, part * 128:(part + 1) * 128]

    def send_rows(step, carry):
        remote(row_parts.at[line], row_parts.at[line], r_send.at[0], r_recv.at[0],
               at_line(step)).start()
        return carry

    lax.fori_loop(1, LINE, send_rows, 0)
    settle(row_parts.at[0:LINE - 1], r_recv.at[0])
    total = row_parts[0]
    for part in range(1, LINE):
        total = total + row_parts[part]
    scale = masses[...].reshape(16, 128) / (total / item_count)
    for at in range(TILES * PARTS):
        user_rows[at] = jnp.broadcast_to(scale[at:at + 1, :], (8, 128))
    column_half[...] = total.reshape(2, 8, 128)
    row_total_ref[...] = column_half[z_lo]

    def sum_columns(unit, column, first):
        for block in range(4):
            pieces = []
            for half in (0, 1):
                acc = jnp.zeros((HALF // 8, 8, 128), F32)
                for tile in range(TILES):
                    for part in range(PARTS):
                        piece = kernel[unit, tile,
                                       block * BLOCK + half * HALF:block * BLOCK + (half + 1) * HALF,
                                       part * 128:(part + 1) * 128]
                        piece = piece.reshape(HALF // 8, 8, 128)
                        acc = acc + piece * user_rows[tile * PARTS + part]
                pieces.append(acc.reshape(HALF, 128))
            flat = jnp.concatenate(pieces, axis=0).T
            column_send[column, first + block] = jnp.sum(flat, axis=0, keepdims=True)

    def column_step(step, carry):
        turn, late = step >> 1, (step & 1) == 1
        column = jnp.where(turn == 0, 3, jnp.where(turn == 3, 0, turn))
        unit = jnp.where(
            late, jnp.where(column == 0, 3, column + 4), jnp.where(column == 3, 4, column)
        )
        sum_columns(unit, column, jnp.where(late, 4, 0))
        for known, done, source, partner in ((1, 3, 3, far), (3, 1, 2, left), (5, 2, 1, right)):
            @pl.when(step == known)
            def _():
                remote(column_send.at[done], column_x.at[source],
                       cx_send.at[0], cx_recv.at[0], partner).start()

        return carry

    lax.fori_loop(0, 8, column_step, 0)
    settle(column_x.at[1:NX], cx_recv.at[0])
    column_x[0] = column_send[0] + column_x[1] + column_x[2] + column_x[3]
    for slot in (7, 5, 6, 3, 4, 1, 2):
        hop = (slot + 1) // 2
        remote(column_x.at[0, slot], column_y.at[slot], cy_send.at[0], cy_recv.at[0],
               at_y(NY - hop if slot % 2 else hop)).start()
    settle(column_y.at[1:NY], cy_recv.at[0])
    total = column_x[0, 0]
    for part in range(1, NY):
        total = total + column_y[part]
    column_total_ref[...] = total

    settle(rows.at[0, 1:NY], y_send.at[0])
    settle(rows.at[1:NX], x_send.at[0])
    for half in (0, 1):
        settle(users.at[half], u_send.at[half])
    settle(masses.at[0], u_send.at[2])
    settle(row_parts.at[0:LINE - 1], r_send.at[0])
    settle(column_y.at[1:NY], cy_send.at[0])
    settle(column_x.at[1:NX], cx_send.at[0])


def on_device(users, items, item_scale, user_mass, item_mass):
    user_count = users.shape[0] * lax.axis_size("wide")
    item_count = items.shape[0] * lax.axis_size("wide") * lax.axis_size("narrow")
    dma = pltpu.SemaphoreType.DMA
    vmem = pl.BlockSpec(memory_space=pltpu.VMEM)
    row_total, column_total = pl.pallas_call(
        functools.partial(body, item_count),
        out_shape=(
            pltpu.VMEM((8, 128), F32),
            pltpu.VMEM((1, 128), F32),
        ),
        in_specs=[pl.BlockSpec(memory_space=pl.ANY)] * 4,
        out_specs=(vmem, vmem),
        scratch_shapes=[
            pltpu.VMEM((USERS, WIDTH), BF16),
            pltpu.VMEM((BLOCK, WIDTH), BF16),
            pltpu.VMEM((1, BLOCK), BF16),
            pltpu.VMEM((NX, NY, BLOCK + 16, WIDTH), BF16),
            pltpu.VMEM((TILES, WIDTH, TILE), BF16),
            pltpu.VMEM((NY, TILES, 4 * BLOCK, TILE), F32),
            pltpu.VMEM((TILES, 8, TILE), F32),
            pltpu.VMEM((LINE, 16, 128), F32),
            pltpu.VMEM((2, 8, 128), F32),
            pltpu.VMEM((TILES * PARTS, 8, 128), F32),
            pltpu.VMEM((NX, NY, 1, BLOCK), F32),
            pltpu.VMEM((NY, 1, BLOCK), F32),
            pltpu.VMEM((NX, NY, 1, BLOCK), F32),
            pltpu.VMEM((2, 8, 128), F32),
            dma((4,)),
            dma((1,)), dma((5,)),
            dma((1,)), dma((5,)),
            dma((4,)),
            dma((3,)), dma((3,)),
            dma((1,)), dma((1,)),
            dma((1,)), dma((1,)),
            dma((1,)), dma((1,)),
        ],
        compiler_params=pltpu.CompilerParams(
            collective_id=0, has_side_effects=True, vmem_limit_bytes=56 * 1024 * 1024
        ),
        cost_estimate=pl.CostEstimate(
            flops=2 * 4096 * 2048 * 256, bytes_accessed=1 << 20, transcendentals=4096 * 2048
        ),
        name="scaling",
    )(users, items, item_scale.reshape(1, 128), user_mass.reshape(8, 128))
    user_scale = user_mass / (row_total.reshape(1024) / item_count)
    item_scale_new = item_mass / (column_total.reshape(128) / user_count)
    return user_scale, item_scale_new


def solution(mesh):
    in_specs = (
        P("wide", None),
        P(("wide", "narrow"), None),
        P(("wide", "narrow")),
        P("wide"),
        P(("wide", "narrow")),
    )
    out_specs = (P("wide"), P(("wide", "narrow")))
    return jax.shard_map(
        on_device, mesh=mesh, in_specs=in_specs, out_specs=out_specs, check_vma=False
    )
```

```python
import functools
import math

import jax
import jax.numpy as jnp
from jax import lax
from jax.experimental import pallas as pl
from jax.experimental.pallas import tpu as pltpu
from jax.sharding import PartitionSpec as P

MESH = pl.DeviceIdType.MESH
F32 = jnp.float32
BF16 = jnp.bfloat16

NX, NY, NZ = 4, 8, 8
LINE = 2 * NZ
BLOCK = 128
USERS = 1024
TILE = 512
TILES = 2 * USERS // TILE
PARTS = TILE // 128
WIDTH = 128
SCALE = 2.0 * math.log2(math.e)


def unit_rows(values, axis):
    squares = jnp.sum(values * values, axis=axis, keepdims=True) + 1e-06
    return (values * lax.rsqrt(squares)).astype(BF16)


def body(
    item_count,
    users_hbm, items_hbm, weight_hbm, mass_hbm,
    row_total_ref, column_total_ref,
    users_in, items_in, weight_in, rows, users, kernel, row_acc, row_parts, masses,
    user_rows, column_send, column_y, column_x, column_half,
    in_sem, x_send, x_recv, y_send, y_recv, f_recv, u_send, u_recv, r_send, r_recv,
    cy_send, cy_recv, cx_send, cx_recv,
):
    wide = lax.axis_index("wide")
    narrow = lax.axis_index("narrow")
    y = wide & (NY - 1)
    x = (wide >> 3) & (NX - 1)
    z_lo = wide >> 5
    line = ((narrow >> 1) << 2) | (z_lo << 1) | (narrow & 1)
    wide_no_y = wide - y
    wide_no_x = wide - (x << 3)
    wide_no_z = wide & (NX * NY - 1)

    def at_x(step):
        return (wide_no_x + (((x + step) & (NX - 1)) << 3), narrow)

    def at_y(step):
        return (wide_no_y + ((y + step) & (NY - 1)), narrow)

    def at_line(step):
        other = (line + step) & (LINE - 1)
        return (wide_no_z + (((other >> 1) & 1) << 5), ((other >> 2) << 1) | (other & 1))

    get_items = pltpu.make_async_copy(items_hbm, items_in, in_sem.at[0])
    get_weight = pltpu.make_async_copy(weight_hbm, weight_in, in_sem.at[1])
    get_users = pltpu.make_async_copy(users_hbm, users_in, in_sem.at[2])
    get_mass = pltpu.make_async_copy(mass_hbm, masses.at[z_lo], in_sem.at[3])
    get_items.start()
    get_weight.start()
    get_users.start()
    get_mass.start()

    barrier = pltpu.get_barrier_semaphore()

    def greet(partner):
        pl.semaphore_signal(barrier, inc=1, device_id=partner, device_id_type=MESH)

    def greet_line(step, carry):
        greet(at_line(step))
        return carry

    for step in (1, 3, 2):
        greet(at_x(step))
    for step in (1, 7, 2, 6, 3, 5, 4):
        greet(at_y(step))
    lax.fori_loop(1, LINE, greet_line, 0)

    get_items.wait()
    get_weight.wait()
    rows[0, 0, 0:BLOCK, :] = unit_rows(items_in[...].astype(F32), 1)
    rows[0, 0, BLOCK:BLOCK + 16, :] = jnp.broadcast_to(
        weight_in[...].astype(F32), (16, BLOCK)
    ).astype(BF16)

    pl.semaphore_wait(barrier, NX - 1 + NY - 1 + LINE - 1)

    def remote(src, dst, send, recv, partner):
        return pltpu.make_async_remote_copy(
            src_ref=src, dst_ref=dst, send_sem=send, recv_sem=recv,
            device_id=partner, device_id_type=MESH,
        )

    def settle(part, sem):
        pltpu.make_async_copy(part, part, sem).wait()

    own = rows.at[0, 0]
    left, right, far = at_x(3), at_x(1), at_x(2)

    def y_send_to(hop):
        if hop == 4:
            remote(own, rows.at[0, 7], y_send.at[0], y_recv.at[4], at_y(4)).start()
            return
        remote(own, rows.at[0, 2 * hop - 1], y_send.at[0], y_recv.at[hop], at_y(hop)).start()
        remote(own, rows.at[0, 2 * hop], y_send.at[0], y_recv.at[hop], at_y(NY - hop)).start()

    def slots_of(hop):
        return slice(2 * hop - 1, 2 * hop + 1) if 0 < hop < 4 else slice(7, 8) if hop else slice(0, 1)

    def x_send_of(hop):
        part = rows.at[0, slots_of(hop)]
        remote(part, rows.at[1, slots_of(hop)], x_send.at[0], x_recv.at[hop], right).start()
        remote(part, rows.at[2, slots_of(hop)], x_send.at[0], x_recv.at[hop], left).start()
        if hop in (0, 4):
            remote(part, rows.at[3, slots_of(hop)], x_send.at[0], x_recv.at[hop], far).start()

    def from_y(hop):
        settle(rows.at[0, slots_of(hop)], y_recv.at[hop])
        x_send_of(hop)

    def from_x(hop):
        if hop in (0, 4):
            settle(rows.at[1:4, slots_of(hop)], x_recv.at[hop])
            return
        settle(rows.at[1:3, slots_of(hop)], x_recv.at[hop])
        behind, ahead = 2 * hop - 1, 2 * hop
        remote(rows.at[1, behind], rows.at[3, behind], x_send.at[0], f_recv.at[hop], right).start()
        remote(rows.at[2, ahead], rows.at[3, ahead], x_send.at[0], f_recv.at[hop], left).start()

    def from_far(hop):
        settle(rows.at[3, slots_of(hop)], f_recv.at[hop])

    y_send_to(1)
    x_send_of(0)
    y_send_to(2)

    up, down = at_line(2), at_line(LINE - 2)
    get_users.wait()
    get_mass.wait()
    for half, partner in ((0, up), (1, down)):
        values = users_in[half * TILE:(half + 1) * TILE, :].T.astype(F32)
        tile = z_lo * 2 + half
        users[tile] = unit_rows(values, 0)
        part = users.at[tile]
        remote(part, part, u_send.at[half], u_recv.at[half], partner).start()
    remote(masses.at[z_lo], masses.at[z_lo], u_send.at[2], u_recv.at[2], up).start()

    from_y(1)
    y_send_to(3)
    y_send_to(4)
    from_y(2)
    row_acc[...] = jnp.zeros_like(row_acc)

    def unit_of(unit):
        late = jnp.logical_or(unit == 3, unit >= 5)
        column = jnp.where(unit < 3, unit, jnp.where(unit == 3, 0, jnp.where(unit == 4, 3, unit - 4)))
        return column, jnp.where(late, 4, 0)

    def spread_weight(column, slot):
        weight = rows[column, slot, BLOCK:BLOCK + 16, :]
        return jnp.concatenate([weight] * (BLOCK // 16), axis=0).T.astype(F32)

    def before(at):
        if at == 2:
            from_x(0)
            from_x(1)
            from_x(2)
        elif at == 3:
            from_y(3)
        elif at == 5:
            from_y(4)
        elif at == 6:
            from_x(3)
        elif at == 8:
            from_far(1)
            from_far(2)
        elif at == 10:
            from_x(4)
        elif at == 14:
            from_far(3)

    def compute_step(at, carry):
        unit, later = at >> 1, at & 1
        column, first = unit_of(unit)
        for known in (2, 3, 5, 6, 8, 10, 14):
            @pl.when(at == known)
            def _():
                before(known)

        @pl.when(at == 1)
        def _():
            for half in (0, 1):
                settle(users.at[half], u_recv.at[half])
            settle(masses.at[0], u_recv.at[2])

        block_of_users = (z_lo + later) & 1
        wide_of = TILE // 2
        accs = [jnp.zeros((8, wide_of), F32) for _ in range(4)]
        for block in range(4):
            left_rows = rows[column, first + block, 0:BLOCK, :]
            weight = spread_weight(column, first + block)
            weight = jnp.concatenate([weight] * (wide_of // 128), axis=1)
            here = slice(block * BLOCK, (block + 1) * BLOCK)
            for part in range(4):
                tile = block_of_users * 2 + part // 2
                there = slice(part % 2 * wide_of, (part % 2 + 1) * wide_of)
                scores = jnp.dot(left_rows, users[tile, :, there], preferred_element_type=F32)
                values = jnp.exp2(scores * SCALE)
                kernel[unit, tile, here, there] = values
                weighted = (values * weight).reshape(BLOCK // 8, 8, wide_of)
                accs[part] += jnp.sum(weighted, axis=0)
        for part in range(4):
            there = slice(part % 2 * wide_of, (part % 2 + 1) * wide_of)
            row_acc[block_of_users * 2 + part // 2, :, there] += accs[part]
        return carry

    lax.fori_loop(0, 16, compute_step, 0)

    for tile in range(TILES):
        total = jnp.sum(row_acc[tile], axis=0, keepdims=True)
        for part in range(PARTS):
            at = tile * PARTS + part
            row_parts[line, at:at + 1, :] = total[:, part * 128:(part + 1) * 128]

    def send_rows(turn, carry):
        off = (turn + 1) >> 1
        step = jnp.where((turn & 1) == 1, NZ - off, NZ + off)
        remote(row_parts.at[line], row_parts.at[line], r_send.at[0], r_recv.at[0],
               at_line(step)).start()
        return carry

    lax.fori_loop(0, LINE - 1, send_rows, 0)
    settle(row_parts.at[0:LINE - 1], r_recv.at[0])
    total = row_parts[0]
    for part in range(1, LINE):
        total = total + row_parts[part]
    scale = masses[...].reshape(16, 128) / (total / item_count)
    for at in range(TILES * PARTS):
        user_rows[at] = jnp.broadcast_to(scale[at:at + 1, :], (8, 128))
    column_half[...] = total.reshape(2, 8, 128)
    row_total_ref[...] = column_half[z_lo]

    def sum_columns(unit, column, first):
        for block in range(4):
            acc = jnp.zeros((BLOCK // 8, 8, 128), F32)
            for tile in range(TILES):
                for part in range(PARTS):
                    piece = kernel[unit, tile, block * BLOCK:(block + 1) * BLOCK,
                                   part * 128:(part + 1) * 128]
                    acc = acc + piece.reshape(BLOCK // 8, 8, 128) * user_rows[tile * PARTS + part]
            flat = acc.reshape(BLOCK, 128).T
            column_send[column, first + block] = jnp.sum(flat, axis=0, keepdims=True)

    def column_step(step, carry):
        turn, late = step >> 1, (step & 1) == 1
        column = jnp.where(turn == 0, 3, jnp.where(turn == 3, 0, turn))
        unit = jnp.where(
            late, jnp.where(column == 0, 3, column + 4), jnp.where(column == 3, 4, column)
        )
        sum_columns(unit, column, jnp.where(late, 4, 0))
        for known, done, source, partner in ((1, 3, 3, far), (3, 1, 2, left), (5, 2, 1, right)):
            @pl.when(step == known)
            def _():
                remote(column_send.at[done], column_x.at[source],
                       cx_send.at[0], cx_recv.at[0], partner).start()

        return carry

    lax.fori_loop(0, 8, column_step, 0)
    settle(column_x.at[1:NX], cx_recv.at[0])
    column_x[0] = column_send[0] + column_x[1] + column_x[2] + column_x[3]
    for slot in (7, 5, 6, 3, 4, 1, 2):
        hop = (slot + 1) // 2
        remote(column_x.at[0, slot], column_y.at[slot], cy_send.at[0], cy_recv.at[0],
               at_y(NY - hop if slot % 2 else hop)).start()
    settle(column_y.at[1:NY], cy_recv.at[0])
    total = column_x[0, 0]
    for part in range(1, NY):
        total = total + column_y[part]
    column_total_ref[...] = total

    settle(rows.at[0, 1:NY], y_send.at[0])
    settle(rows.at[1:NX], x_send.at[0])
    for half in (0, 1):
        settle(users.at[half], u_send.at[half])
    settle(masses.at[0], u_send.at[2])
    settle(row_parts.at[0:LINE - 1], r_send.at[0])
    settle(column_y.at[1:NY], cy_send.at[0])
    settle(column_x.at[1:NX], cx_send.at[0])


def on_device(users, items, item_scale, user_mass, item_mass):
    user_count = users.shape[0] * lax.axis_size("wide")
    item_count = items.shape[0] * lax.axis_size("wide") * lax.axis_size("narrow")
    dma = pltpu.SemaphoreType.DMA
    vmem = pl.BlockSpec(memory_space=pltpu.VMEM)
    row_total, column_total = pl.pallas_call(
        functools.partial(body, item_count),
        out_shape=(
            pltpu.VMEM((8, 128), F32),
            pltpu.VMEM((1, 128), F32),
        ),
        in_specs=[pl.BlockSpec(memory_space=pl.ANY)] * 4,
        out_specs=(vmem, vmem),
        scratch_shapes=[
            pltpu.VMEM((USERS, WIDTH), BF16),
            pltpu.VMEM((BLOCK, WIDTH), BF16),
            pltpu.VMEM((1, BLOCK), BF16),
            pltpu.VMEM((NX, NY, BLOCK + 16, WIDTH), BF16),
            pltpu.VMEM((TILES, WIDTH, TILE), BF16),
            pltpu.VMEM((NY, TILES, 4 * BLOCK, TILE), F32),
            pltpu.VMEM((TILES, 8, TILE), F32),
            pltpu.VMEM((LINE, 16, 128), F32),
            pltpu.VMEM((2, 8, 128), F32),
            pltpu.VMEM((TILES * PARTS, 8, 128), F32),
            pltpu.VMEM((NX, NY, 1, BLOCK), F32),
            pltpu.VMEM((NY, 1, BLOCK), F32),
            pltpu.VMEM((NX, NY, 1, BLOCK), F32),
            pltpu.VMEM((2, 8, 128), F32),
            dma((4,)),
            dma((1,)), dma((5,)),
            dma((1,)), dma((5,)),
            dma((4,)),
            dma((3,)), dma((3,)),
            dma((1,)), dma((1,)),
            dma((1,)), dma((1,)),
            dma((1,)), dma((1,)),
        ],
        compiler_params=pltpu.CompilerParams(
            collective_id=0, has_side_effects=True, vmem_limit_bytes=56 * 1024 * 1024
        ),
        cost_estimate=pl.CostEstimate(
            flops=2 * 4096 * 2048 * 256, bytes_accessed=1 << 20, transcendentals=4096 * 2048
        ),
        name="scaling",
    )(users, items, item_scale.reshape(1, 128), user_mass.reshape(8, 128))
    user_scale = user_mass / (row_total.reshape(1024) / item_count)
    item_scale_new = item_mass / (column_total.reshape(128) / user_count)
    return user_scale, item_scale_new


def solution(mesh):
    in_specs = (
        P("wide", None),
        P(("wide", "narrow"), None),
        P(("wide", "narrow")),
        P("wide"),
        P(("wide", "narrow")),
    )
    out_specs = (P("wide"), P(("wide", "narrow")))
    return jax.shard_map(
        on_device, mesh=mesh, in_specs=in_specs, out_specs=out_specs, check_vma=False
    )
```
